32 devices in a mesh: groups: 2 (over y), blk: 8 (over z, x), uly: 2 (over core).
Axes of the slice: x: 2, y: 2, z: 4, core: 2. Of those that a mesh axis runs over, the one named last changes fastest.
Arguments:
- query: bfloat16 [4096, 1536], P(('groups', 'blk', 'uly')), parts along dimension 0, may hold values from -12 to 12
- key: bfloat16 [4096, 1536], P(('groups', 'blk', 'uly')), parts along dimension 0, may hold values from -6 to 6
- value: bfloat16 [4096, 1536], P(('groups', 'blk', 'uly')), parts along dimension 0, may hold values from -6 to 6
- keep: int32 [64, 28], P(('groups', 'blk')), parts along dimension 0, may hold values from 0 to 1, as said below
Outputs:
- attended: bfloat16 [4096, 1536], P(('groups', 'blk', 'uly')), parts along dimension 0
The draws below stay inside these ranges and needn't reach their ends.
There are 2 independent parts, one for each index of `groups`. The reference program is written for one: setup_inputs(seed, part) draws one part's arguments, and reference() takes and returns one part's arrays. A program takes and returns all parts, laid end to end along the dimension named above; each array names one. Nothing has to cross between parts.
Inputs may be any that keep to these rules, and one draw needn't show every extreme that they name: Tile i has coordinates (i // 8, (i // 2) % 4, i % 2) in the clip's grid of tiles. keep[i, j] refers to key tile (i // 4 - 3) * 4 + j; it is 0 where that tile lies outside the clip, 1 where it is tile i itself, and otherwise 1 exactly when each coordinate differs from tile i's by no more than a per-tile reach of 0 or 1 in that coordinate.
All inputs are finite; a program needn't handle non-finite values.
Results may differ from the reference program's by a relative error of at most 0.0029.
Values may be sent and summed in bfloat16 or wider, within the bound.
No kernel may reach another device: no remote copies, remote signals or barrier semaphores. Data moves between devices by JAX's collectives and lax.ppermute only.
A program may use at most 64 MiB of HBM per device.

```python
import math
import jax
import jax.numpy as jnp
from jax import lax

HEADS = 12
HD = 128
TILE = 64
TH = 4
TW = 2
QBLK = 256
TILES_BLK = 4
RADIUS = 3
BAND = 28
SEQ = 2048
NTILES = 32
N_BLK = 8


def draw_query(key, part):
    noise_key = jax.random.fold_in(key, 1)
    base = jnp.clip(3.0 * jax.random.normal(noise_key, (SEQ, HEADS * HD), jnp.float32), -12.0, 12.0)
    return base.astype(jnp.bfloat16)


def draw_key(key, part):
    noise_key = jax.random.fold_in(key, 2)
    base = jnp.clip(jax.random.normal(noise_key, (SEQ, HEADS * HD), jnp.float32), -6.0, 6.0)
    return base.astype(jnp.bfloat16)


def draw_keep(key, part):
    tiles = jnp.arange(NTILES, dtype=jnp.int32)[:, None]
    column = jnp.arange(BAND, dtype=jnp.int32)[None, :]
    other = (tiles // TILES_BLK - RADIUS) * TILES_BLK + column
    reaches = jax.random.randint(jax.random.fold_in(key, 3), (3, NTILES, 1), 0, 2)
    plane = TH * TW
    near_t = jnp.abs(tiles // plane - other // plane) <= reaches[0]
    near_h = jnp.abs(tiles // TW % TH - other // TW % TH) <= reaches[1]
    near_w = jnp.abs(tiles % TW - other % TW) <= reaches[2]
    inside = (other >= 0) & (other < NTILES)
    return (near_t & near_h & near_w & inside).astype(jnp.int32)


def shard_levels(own_key, extent, shards, smallest, largest):
    factor_of, own = 1.0, jax.random.fold_in(own_key, 6)
    for dim, blocks in shards:
        steps = jnp.exp(jax.random.uniform(jax.random.fold_in(own, dim), (blocks,), jnp.float32, smallest / len(shards), largest / len(shards)))
        factor_of = factor_of * jnp.repeat(steps, extent[dim] // blocks).reshape([-1 if axis == dim else 1 for axis in range(len(extent))])
    return factor_of


def scatter_about(key, dims, width, limit, shards=(), held_as=jnp.bfloat16):
    level = shard_levels(key, dims, shards, -0.22, 0.18) if shards else 1.0
    drawn = jax.random.normal(key, dims, jnp.float32) * width * level
    return jnp.minimum(jnp.maximum(drawn, -limit), limit).astype(held_as)


def setup_inputs(seed: int = 0, part: int = 0) -> dict:
    splits = jax.random.split(jax.random.key(seed), 5)
    part_splits = jax.random.split(jax.random.fold_in(splits[4], part), 5)
    query = draw_query(jax.random.fold_in(jax.random.fold_in(splits[4], part), 71), part)
    key = draw_key(jax.random.fold_in(jax.random.fold_in(splits[4], part), 71), part)
    value = scatter_about(part_splits[2], (SEQ, HEADS * HD), 1.0, 6.0, ((0, 16),))
    keep = draw_keep(jax.random.fold_in(jax.random.fold_in(splits[4], part), 71), part)
    return {"query": query, "key": key, "value": value, "keep": keep}


def reference(query, key, value, keep):
    scale = 1.0 / math.sqrt(HD)
    span = (2 * RADIUS + 1) * QBLK
    q_all = query.reshape(N_BLK, QBLK, HEADS, HD)
    padding = ((RADIUS * QBLK, RADIUS * QBLK), (0, 0))
    k_pad = jnp.pad(key, padding)
    v_pad = jnp.pad(value, padding)
    flags = keep.reshape(N_BLK, TILES_BLK, BAND)

    def one_block(block):
        q_blk = lax.dynamic_index_in_dim(q_all, block, 0, keepdims=False).astype(jnp.float32)
        begin = (block * QBLK).astype(jnp.int32)
        k_blk = lax.dynamic_slice_in_dim(k_pad, begin, span, 0).reshape(span, HEADS, HD).astype(jnp.float32)
        v_blk = lax.dynamic_slice_in_dim(v_pad, begin, span, 0).reshape(span, HEADS, HD).astype(jnp.float32)
        tile_flags = lax.dynamic_index_in_dim(flags, block, 0, keepdims=False) > 0
        mask = jnp.repeat(jnp.repeat(tile_flags, TILE, axis=0), TILE, axis=1)[:, None, :]
        scores = jnp.einsum('qhd,khd->qhk', q_blk, k_blk) * scale
        masked = jnp.where(mask, scores, -1e+30)
        peak = lax.optimization_barrier(jnp.max(masked, axis=2, keepdims=True))
        weights = jnp.where(mask, jnp.exp(masked - peak), 0.0)
        total = lax.optimization_barrier(jnp.sum(weights, axis=2))
        rounded = lax.optimization_barrier(weights.astype(jnp.bfloat16)).astype(jnp.float32)
        mixed = jnp.einsum('qhk,khd->qhd', rounded, v_blk) / total[:, :, None]
        return mixed.astype(jnp.bfloat16).reshape(QBLK, HEADS * HD)
    result = lax.map(one_block, jnp.arange(N_BLK, dtype=jnp.int32))
    return result.reshape(SEQ, HEADS * HD)
```

```python
import functools
import math

import jax
import jax.numpy as jnp
from jax import lax
from jax.experimental import pallas as pl
from jax.experimental.pallas import tpu as pltpu
from jax.sharding import PartitionSpec as P

HD = 128
TILE = 64
TH = 4
TW = 2
HEADS_STEP = 2
FILL = -1e30
LOG2E = 1.4426950408889634


def plane_pairs(n_blk, n_uly, parity):
    rows = TH // n_uly
    planes = n_blk // rows
    route = []
    for blk in range(n_blk):
        t = blk // rows
        other = t + 1 if t % 2 == parity else t - 1
        for u in range(n_uly):
            if 0 <= other < planes:
                there = (other * rows + blk % rows) * n_uly + u
            else:
                there = blk * n_uly + n_uly - 1 - u
            route.append((blk * n_uly + u, there))
    return route


def row_pairs(n_groups, n_blk, n_uly):
    route = []
    size = n_blk * n_uly
    for g in range(n_groups):
        for i in range(size):
            h = i % TH
            if h == 1:
                there = g * size + i + 1
            elif h == 2:
                there = g * size + i - 1
            else:
                there = (g + 1) % n_groups * size + i
            route.append((g * size + i, there))
    return route


def scores_kernel(meta, keep_own, keep_x, q_own, q_d, q_x, k_own, k_e, k_o, p_ref, st_own, st_d, st_x, bias):
    scale = LOG2E / math.sqrt(HD)
    parity, xh, u, inner = meta[0], meta[1], meta[2], meta[3]
    step = 1 - 2 * parity

    @pl.when(pl.program_id(0) == 0)
    def _():
        first = lax.broadcasted_iota(jnp.int32, (1, HD), 1) < TILE
        for src in range(3):
            table = keep_x if src == 2 else keep_own
            row = TW * (u if src == 0 else 1 - u)
            half = (1 - xh) if src == 2 else xh
            for n, dt in enumerate((0, step, -step)):
                column = TH * TW * dt + TW * (2 * xh + u) - 2 * TW * half + 12
                for w in range(TW):
                    col = jnp.clip(column + w, 0, keep_own.shape[1] - 1)
                    low = jnp.where(table[row, col] > 0, 0.0, FILL)
                    high = jnp.where(table[row + 1, col] > 0, 0.0, FILL)
                    bias[pl.ds((src * 3 + n) * TW + w, 1), :] = jnp.where(first, low, high)

    def one(src, i, q_ref, st_ref):
        cols = pl.ds(i * HD, HD)
        q = q_ref[:, cols]
        parts = []
        for n, k_ref in enumerate((k_own, k_e, k_o)):
            s = lax.dot_general(k_ref[:, cols], q, (((1,), (1,)), ((), ())), preferred_element_type=jnp.float32)
            for w in range(TW):
                b = bias[pl.ds((src * 3 + n) * TW + w, 1), :]
                parts.append(s[w * TILE : (w + 1) * TILE] * scale + b)
        t = jnp.concatenate(parts, axis=0)
        m = jnp.max(t, axis=0, keepdims=True)
        e = jnp.exp2(t - m)
        total = jnp.sum(e, axis=0, keepdims=True)
        p_ref[i, :, src * HD : (src + 1) * HD] = e.astype(jnp.bfloat16)
        st_ref[0, pl.ds(i, 1), :] = m
        st_ref[0, pl.ds(HEADS_STEP + i, 1), :] = total

    for i in range(HEADS_STEP):
        one(0, i, q_own, st_own)
        one(1, i, q_d, st_d)

    @pl.when(inner == 1)
    def _():
        for i in range(HEADS_STEP):
            one(2, i, q_x, st_x)


def values_kernel(p_ref, v_own, v_e, v_o, st_own, st_d, st_x, o_own, o_d, o_x):
    for i in range(HEADS_STEP):
        cols = pl.ds(i * HD, HD)
        v = jnp.concatenate([v_own[:, cols], v_e[:, cols], v_o[:, cols]], axis=0)
        acc = lax.dot_general(v, p_ref[i], (((0,), (0,)), ((), ())), preferred_element_type=jnp.float32)
        for src, (o_ref, st) in enumerate(((o_own, st_own), (o_d, st_d), (o_x, st_x))):
            total = st[0, pl.ds(HEADS_STEP + i, 1), :]
            o_ref[cols, :] = (acc[:, src * HD : (src + 1) * HD] / total).astype(o_ref.dtype)


def combine_kernel(meta, o_own, o_d, o_x, st_own, st_d, st_x, out):
    inner = meta[3] == 1
    m0, l0 = st_own[0, :HEADS_STEP], st_own[0, HEADS_STEP:]
    m1, l1 = st_d[0, :HEADS_STEP], st_d[0, HEADS_STEP:]
    m2 = jnp.where(inner, st_x[0, :HEADS_STEP], FILL)
    l2 = jnp.where(inner, st_x[0, HEADS_STEP:], 0.0)
    peak = jnp.maximum(jnp.maximum(m0, m1), m2)
    f0, f1, f2 = l0 * jnp.exp2(m0 - peak), l1 * jnp.exp2(m1 - peak), l2 * jnp.exp2(m2 - peak)
    total = f0 + f1 + f2
    w0, w1, w2 = f0 / total, f1 / total, f2 / total
    for i in range(HEADS_STEP):
        cols = pl.ds(i * HD, HD)
        o = o_own[cols, :] * w0[i : i + 1] + o_d[cols, :].astype(jnp.float32) * w1[i : i + 1]
        x = jnp.where(inner, o_x[cols, :].astype(jnp.float32), 0.0)
        o = o + x * w2[i : i + 1]
        out[:, cols] = o.T.astype(out.dtype)


def body(n_groups, query, key, value, keep):
    n_blk, n_uly = lax.axis_size("blk"), lax.axis_size("uly")
    rows, width = query.shape
    heads = width // HD
    steps = heads // HEADS_STEP
    axes = ("blk", "uly")
    everyone = ("groups", "blk", "uly")
    even, odd = plane_pairs(n_blk, n_uly, 0), plane_pairs(n_blk, n_uly, 1)
    cross = row_pairs(n_groups, n_blk, n_uly)
    cores = [(0, 1), (1, 0)]
    halves = [(b, b ^ 1) for b in range(n_blk)]

    blk, u = lax.axis_index("blk"), lax.axis_index("uly")
    xh = blk % 2
    meta = jnp.stack([blk // 2 % 2, xh, u, (xh != u).astype(jnp.int32)]).astype(jnp.int32)

    k_e = lax.ppermute(key, axes, even)
    k_o = lax.ppermute(key, axes, odd)
    keep_x = lax.ppermute(keep, "blk", halves)
    q_x = lax.ppermute(query, everyone, cross)
    q_d = lax.ppermute(query, "uly", cores)
    v_e = lax.ppermute(value, axes, even)
    v_o = lax.ppermute(value, axes, odd)

    smem = pl.BlockSpec(memory_space=pltpu.SMEM)
    feat = pl.BlockSpec((rows, HEADS_STEP * HD), lambda g: (0, g))
    tall = pl.BlockSpec((HEADS_STEP * HD, rows), lambda g: (g, 0))
    stat = pl.BlockSpec((1, 2 * HEADS_STEP, rows), lambda g: (g, 0, 0))
    prob = pl.BlockSpec((HEADS_STEP, 3 * rows, 3 * rows), lambda g: (g, 0, 0))
    stat_shape = jax.ShapeDtypeStruct((steps, 2 * HEADS_STEP, rows), jnp.float32)

    p, st_own, st_d, st_x = pl.pallas_call(
        scores_kernel,
        grid=(steps,),
        in_specs=[smem, smem, smem] + [feat] * 6,
        out_specs=[prob, stat, stat, stat],
        out_shape=[jax.ShapeDtypeStruct((heads, 3 * rows, 3 * rows), jnp.bfloat16), stat_shape, stat_shape, stat_shape],
        scratch_shapes=[pltpu.VMEM((24, HD), jnp.float32)],
        name="scores",
    )(meta, keep, keep_x, query, q_d, q_x, key, k_e, k_o)

    in_d = lax.ppermute(st_d, "uly", cores)
    in_x = lax.ppermute(st_x, everyone, cross)

    o_own, o_d, o_x = pl.pallas_call(
        values_kernel,
        grid=(steps,),
        in_specs=[prob, feat, feat, feat, stat, stat, stat],
        out_specs=[tall, tall, tall],
        out_shape=[
            jax.ShapeDtypeStruct((width, rows), jnp.float32),
            jax.ShapeDtypeStruct((width, rows), jnp.bfloat16),
            jax.ShapeDtypeStruct((width, rows), jnp.bfloat16),
        ],
        name="values",
    )(p, value, v_e, v_o, st_own, st_d, st_x)

    back_x = lax.ppermute(o_x, everyone, cross)
    back_d = lax.ppermute(o_d, "uly", cores)

    return pl.pallas_call(
        combine_kernel,
        grid=(steps,),
        in_specs=[smem, tall, tall, tall, stat, stat, stat],
        out_specs=feat,
        out_shape=jax.ShapeDtypeStruct((rows, width), query.dtype),
        name="combine",
    )(meta, o_own, back_d, back_x, st_own, in_d, in_x)


def solution(mesh):
    tokens = P(("groups", "blk", "uly"), None)
    return jax.shard_map(
        functools.partial(body, mesh.shape["groups"]),
        mesh=mesh,
        in_specs=(tokens, tokens, tokens, P(("groups", "blk"), None)),
        out_specs=tokens,
        check_vma=False,
    )
```

```python
import functools
import math

import jax
import jax.numpy as jnp
from jax import lax
from jax.experimental import pallas as pl
from jax.experimental.pallas import tpu as pltpu
from jax.sharding import PartitionSpec as P

HD = 128
TILE = 64
TH = 4
TW = 2
HEADS_STEP = 2
STAT = 16
FLAG_ROWS = 16
FILL = -1e30
LOG2E = 1.4426950408889634


def plane_pairs(n_blk, n_uly, parity):
    blks = TH // n_uly
    route = []
    for blk in range(n_blk):
        t = blk // blks
        other = t + 1 if t % 2 == parity else t - 1
        for u in range(n_uly):
            there = blk, n_uly - 1 - u
            if 0 <= other < n_blk // blks:
                there = other * blks + blk % blks, u
            route.append((blk * n_uly + u, there[0] * n_uly + there[1]))
    return route


def row_pairs(n_groups, n_blk, n_uly):
    route = []
    size = n_blk * n_uly
    for g in range(n_groups):
        for i in range(size):
            h = i % TH
            if h == 1:
                there = g * size + i + 1
            elif h == 2:
                there = g * size + i - 1
            else:
                there = (g + 1) % n_groups * size + i
            route.append((g * size + i, there))
    return route


def place():
    n_uly = lax.axis_size("uly")
    rows = TH // n_uly
    blk = lax.axis_index("blk")
    row = lax.rem(blk, rows) * n_uly + lax.axis_index("uly")
    return lax.rem(lax.div(blk, rows), 2), row, (row > 0) & (row < TH - 1)


def flag_rows(keep, parity, key_row, query_row):
    first = lax.broadcasted_iota(jnp.int32, (1, HD), 1) < TILE
    tiles = keep.shape[0]
    line = lax.rem(query_row * TW, tiles)
    base = (keep.shape[1] - tiles) // 2
    step = 1 - 2 * parity
    rows = []
    for dt in (0, step, -step):
        column = base + TH * TW * dt + TW * (key_row - query_row) + line
        for w in range(TW):
            col = jnp.clip(column + w, 0, keep.shape[1] - 1)
            low = (keep[line, col] > 0).astype(jnp.float32)
            high = (keep[line + 1, col] > 0).astype(jnp.float32)
            rows.append(jnp.where(first, low, high))
    return rows


def prepare_kernel(keep_hbm, q_hbm, bias, q_out, keep, sems):
    tokens = q_hbm.shape[0]
    flags = pltpu.make_async_copy(keep_hbm, keep, sems.at[0])
    flags.start()
    copy = pltpu.make_async_copy(q_hbm, q_out.at[:tokens], sems.at[1])
    copy.start()
    flags.wait()
    parity, row, _ = place()
    sibling = row + 1 - 2 * lax.rem(row, 2)
    across = jnp.where(row < TH // 2, row + 1, row - 1)
    rows = flag_rows(keep, parity, row, row) + flag_rows(keep, parity, row, sibling)
    rows += [jnp.ones((1, HD), jnp.float32)] * (bias.shape[0] - len(rows))
    bias[...] = (jnp.concatenate(rows, axis=0) - 1.0) * -FILL
    rows = flag_rows(keep, parity, across, row)
    rows += [jnp.zeros((1, HD), jnp.float32)] * (FLAG_ROWS - len(rows))
    q_out[tokens:, :HD] = jnp.concatenate(rows, axis=0).astype(q_out.dtype)
    copy.wait()


def unit(h, q_ref, k_ref, flags, p_ref, st_ref, src):
    scale = LOG2E / math.sqrt(HD)
    cols = pl.ds(pl.multiple_of(h * HD, HD), HD)
    s = lax.dot_general(
        k_ref[:, cols], q_ref[: k_ref.shape[0], cols], (((1,), (1,)), ((), ())), preferred_element_type=jnp.float32
    )
    t = jnp.concatenate([s[w * TILE : (w + 1) * TILE] * scale + flags[w] for w in range(TW)], axis=0)
    m = jnp.max(t, axis=0, keepdims=True)
    e = jnp.exp2(t - m)
    p_ref[h, :, src * HD : (src + 1) * HD] = e.astype(jnp.bfloat16)
    st_ref[src, pl.ds(h, 1), :] = m
    st_ref[src, pl.ds(STAT + h, 1), :] = jnp.sum(e, axis=0, keepdims=True)


def all_heads(p_ref, units):
    def step(j, _):
        for i in range(HEADS_STEP):
            for args in units:
                unit(j * HEADS_STEP + i, *args)
        return 0

    lax.fori_loop(0, p_ref.shape[0] // HEADS_STEP, step, 0)


def bias_rows(bias, src, plane):
    at = (src * 3 + plane) * TW
    return [bias[at + w : at + w + 1, :] for w in range(TW)]


def own_scores_kernel(bias, k_hbm, v_hbm, q_own, q_d, p_d, st_d, k_own, v_a, v_b, sems):
    copies = [
        pltpu.make_async_copy(k_hbm, k_own, sems.at[0]),
        pltpu.make_async_copy(v_hbm.at[:, : v_a.shape[1]], v_a, sems.at[1]),
        pltpu.make_async_copy(v_hbm.at[:, v_a.shape[1] :], v_b, sems.at[2]),
    ]
    for copy in copies:
        copy.start()
    st_d[...] = jnp.ones_like(st_d)
    for copy in copies:
        copy.wait()
    all_heads(
        p_d,
        [
            (q_own, k_own, bias_rows(bias, 0, 0), p_d, st_d, 0),
            (q_d, k_own, bias_rows(bias, 1, 0), p_d, st_d, 1),
        ],
    )


def near_scores_kernel(bias, k_e, k_o, q_own, q_d, p_1, st_1, p_2, st_2):
    units = []
    for plane, k_ref, p_ref, st_ref in ((1, k_e, p_1, st_1), (2, k_o, p_2, st_2)):
        st_ref[...] = jnp.ones_like(st_ref)
        units += [(q, k_ref, bias_rows(bias, src, plane), p_ref, st_ref, src) for src, q in enumerate((q_own, q_d))]
    all_heads(p_1, units)


def far_scores_kernel(k_own, k_e, k_o, q_x, p_0, st_0, p_1, st_1, p_2, st_2):
    _, _, inner = place()

    @pl.when(inner)
    def _():
        tokens = k_own.shape[0]
        flags = [q_x[tokens + r : tokens + r + 1, :HD].astype(jnp.float32) for r in range(3 * TW)]
        units = []
        for plane, k_ref, p_ref, st_ref in ((0, k_own, p_0, st_0), (1, k_e, p_1, st_1), (2, k_o, p_2, st_2)):
            st_ref[...] = jnp.ones_like(st_ref)
            rows = [(f - 1.0) * -FILL for f in flags[plane * TW : (plane + 1) * TW]]
            units.append((q_x, k_ref, rows, p_ref, st_ref, 0))
        all_heads(p_0, units)


def merge(stats, src):
    peaks = [st[src, :STAT] for st in stats]
    sums = [st[src, STAT:] for st in stats]
    peak = functools.reduce(jnp.maximum, peaks)
    factors = [jnp.exp2(m - peak) for m in peaks]
    total = sum(f * v for f, v in zip(factors, sums))
    return peak, total, [f / total for f in factors]


def mix(heads, ps, vs, factors, outs):
    for n, h in enumerate(heads):
        cols = pl.ds(n * HD, HD)
        dots = [
            lax.dot_general(v[:, cols], p[h], (((0,), (0,)), ((), ())), preferred_element_type=jnp.float32)
            for p, v in zip(ps, vs)
        ]
        for src, out in enumerate(outs):
            part = [d[:, src * HD : (src + 1) * HD] * f[h : h + 1] for d, f in zip(dots, factors[src])]
            out[cols, :] = (part[0] + part[1] + part[2]).astype(out.dtype)


def put_split(o_ref, at, values, pieces):
    for _ in range(pieces):
        piece = values.astype(jnp.bfloat16)
        o_ref[at : at + STAT, :] = piece
        values = values - piece.astype(jnp.float32)
        at += STAT


def get_split(o_ref, at, pieces):
    return sum(o_ref[at + n * STAT : at + (n + 1) * STAT, :].astype(jnp.float32) for n in range(pieces))


def far_values_kernel(heads, p0, p1, p2, s0, s1, s2, v_own, v_e, v_o, o_x):
    _, _, inner = place()

    @pl.when(inner)
    def _():
        peak, total, factors = merge((s0, s1, s2), 0)
        mix(heads, (p0, p1, p2), (v_own, v_e, v_o), [factors], [o_x])
        if heads[0] == 0:
            put_split(o_x, len(heads) * HD, peak, 3)
        else:
            put_split(o_x, len(heads) * HD, total, 2)


def near_values_kernel(heads, p0, p1, p2, s0, s1, s2, v_own, v_e, v_o, o_own, o_d, *st_own):
    peak, total, own = merge((s0, s1, s2), 0)
    for ref in st_own:
        ref[:STAT] = peak
        ref[STAT:] = total
    peak, total, sib = merge((s0, s1, s2), 1)
    if heads[0] == 0:
        put_split(o_d, len(heads) * HD, peak, 3)
        put_split(o_d, (len(heads) * HD) + 3 * STAT, total, 2)
    mix(heads, (p0, p1, p2), (v_own, v_e, v_o), [own, sib], [o_own, o_d])


def combine_kernel(own_a, own_b, xa, xb, da, db, st_own, out):
    _, _, inner = place()

    wide_a, wide_b = own_a.shape[0], own_b.shape[0]
    m0, l0 = st_own[:STAT], st_own[STAT:]
    m1, l1 = get_split(da, wide_a, 3), get_split(da, wide_a + 3 * STAT, 2)
    m2, l2 = get_split(xa, wide_a, 3), get_split(xb, wide_b, 2)
    m2, l2 = jnp.where(inner, m2, FILL), jnp.where(inner, l2, 0.0)
    peak = jnp.maximum(jnp.maximum(m0, m1), m2)
    f0, f1, f2 = l0 * jnp.exp2(m0 - peak), l1 * jnp.exp2(m1 - peak), l2 * jnp.exp2(m2 - peak)
    total = f0 + f1 + f2
    w0, w1, w2 = f0 / total, f1 / total, f2 / total
    h = 0
    for o_own, o_x, o_d in ((own_a, xa, da), (own_b, xb, db)):
        for n in range(o_own.shape[0] // HD):
            cols = pl.ds(n * HD, HD)
            x = jnp.where(inner, o_x[cols, :].astype(jnp.float32), 0.0)
            o = o_own[cols, :] * w0[h : h + 1] + o_d[cols, :].astype(jnp.float32) * w1[h : h + 1] + x * w2[h : h + 1]
            out[:, pl.ds(h * HD, HD)] = o.T.astype(out.dtype)
            h += 1


def body(n_groups, query, key, value, keep):
    n_blk, n_uly = lax.axis_size("blk"), lax.axis_size("uly")
    rows, width = query.shape
    heads = width // HD
    first = heads * 2 // 3
    heads_a, heads_b = range(first), range(first, heads)
    wide_a, wide_b = first * HD, width - first * HD
    everyone = ("groups", "blk", "uly")
    cross = row_pairs(n_groups, n_blk, n_uly)
    cores = [(0, 1), (1, 0)]
    vmem = pl.BlockSpec(memory_space=pltpu.VMEM)
    hbm = pl.BlockSpec(memory_space=pltpu.HBM)
    bf16, f32 = jnp.bfloat16, jnp.float32

    def exchange(x, parity):
        return lax.ppermute(x, ("blk", "uly"), plane_pairs(n_blk, n_uly, parity))

    def call(kernel, name, us, in_specs, out_shape, scratch=()):
        return pl.pallas_call(
            kernel,
            in_specs=in_specs,
            out_specs=jax.tree.map(lambda _: vmem, out_shape),
            out_shape=out_shape,
            scratch_shapes=scratch,
            compiler_params=pltpu.CompilerParams(vmem_limit_bytes=16 * 1024 * 1024),
            cost_estimate=pl.CostEstimate(flops=int(us * 1e9), bytes_accessed=0, transcendentals=0),
            name=name,
        )

    def array(dtype, *shape):
        return jax.ShapeDtypeStruct(shape, dtype)

    p_near, s_near = array(bf16, heads, rows, 2 * rows), array(f32, 2, 2 * STAT, rows)
    p_far, s_far = array(bf16, heads, rows, rows), array(f32, 1, 2 * STAT, rows)
    far_a, far_b = array(bf16, wide_a + 3 * STAT, rows), array(bf16, wide_b + 2 * STAT, rows)
    near_a, near_b = array(bf16, wide_a + 5 * STAT, rows), array(bf16, wide_b, rows)

    k_e = exchange(key, 0)
    k_o = exchange(key, 1)
    q_d = lax.ppermute(query, "uly", cores)
    q_late, _ = lax.optimization_barrier((query, q_d))
    near, q_own = call(
        prepare_kernel,
        "prepare",
        0.7,
        [hbm, hbm],
        [array(f32, 16, HD), array(bf16, rows + FLAG_ROWS, width)],
        [pltpu.SMEM(keep.shape, keep.dtype), pltpu.SemaphoreType.DMA((2,))],
    )(keep, q_late)
    q_x = lax.ppermute(q_own, everyone, cross)

    pd0, sd0, k_own, v_a, v_b = call(
        own_scores_kernel,
        "own_scores",
        1.5,
        [vmem, hbm, hbm, vmem, vmem],
        [p_near, s_near, array(bf16, rows, width), array(bf16, rows, wide_a), array(bf16, rows, wide_b)],
        [pltpu.SemaphoreType.DMA((3,))],
    )(near, key, value, q_own, q_d)

    va_e = exchange(v_a, 0)
    va_o = exchange(v_a, 1)
    v_last, k_e, k_o, _ = lax.optimization_barrier((v_b, k_e, k_o, sd0))
    vb_e = exchange(v_last, 0)
    vb_o = exchange(v_last, 1)

    pd1, sd1, pd2, sd2 = call(near_scores_kernel, "near_scores", 2, [vmem] * 5, [p_near, s_near] * 2)(
        near, k_e, k_o, q_own, q_d
    )
    q_x, _ = lax.optimization_barrier((q_x, sd2))
    px0, sx0, px1, sx1, px2, sx2 = call(far_scores_kernel, "far_scores", 0, [vmem] * 4, [p_far, s_far] * 3)(
        k_own, k_e, k_o, q_x
    )
    va_e, va_o, _ = lax.optimization_barrier((va_e, va_o, sx2))
    far = px0, px1, px2, sx0, sx1, sx2
    nigh = pd0, pd1, pd2, sd0, sd1, sd2

    xa = call(functools.partial(far_values_kernel, heads_a), "far_values_a", 2, [vmem] * 9, far_a)(
        *far, v_a, va_e, va_o
    )
    back_xa = lax.ppermute(xa, everyone, cross)
    va_e, va_o, _ = lax.optimization_barrier((va_e, va_o, xa))
    own_a, da, s_own = call(
        functools.partial(near_values_kernel, heads_a),
        "near_values_a",
        2,
        [vmem] * 9,
        [array(f32, wide_a, rows), near_a, array(f32, 2 * STAT, rows)],
    )(*nigh, v_a, va_e, va_o)
    back_da = lax.ppermute(da, "uly", cores)

    vb_e, vb_o, _, _ = lax.optimization_barrier((vb_e, vb_o, s_own, xa))
    xb = call(functools.partial(far_values_kernel, heads_b), "far_values_b", 5, [vmem] * 9, far_b)(
        *far, v_b, vb_e, vb_o
    )
    back_xb = lax.ppermute(xb, everyone, cross)
    own_b, db = call(
        functools.partial(near_values_kernel, heads_b), "near_values_b", 5, [vmem] * 9, [array(f32, wide_b, rows), near_b]
    )(*nigh, v_b, vb_e, vb_o)
    back_db = lax.ppermute(db, "uly", cores)

    return call(combine_kernel, "combine", 0, [vmem] * 7, array(query.dtype, rows, width))(
        own_a, own_b, back_xa, back_xb, back_da, back_db, s_own
    )


def solution(mesh):
    tokens = P(("groups", "blk", "uly"), None)
    return jax.shard_map(
        functools.partial(body, mesh.shape["groups"]),
        mesh=mesh,
        in_specs=(tokens, tokens, tokens, P(("groups", "blk"), None)),
        out_specs=tokens,
        check_vma=False,
    )
```

```python
import functools
import math

import jax
import jax.numpy as jnp
from jax import lax
from jax.experimental import pallas as pl
from jax.experimental.pallas import tpu as pltpu
from jax.sharding import PartitionSpec as P

HD = 128
TILE = 64
TH = 4
TW = 2
STAT = 16
FLAG_ROWS = 16
FILL = -1e30
LOG2E = 1.4426950408889634


def plane_pairs(n_blk, n_uly, parity):
    blks = TH // n_uly
    route = []
    for blk in range(n_blk):
        t = blk // blks
        other = t + 1 if t % 2 == parity else t - 1
        for u in range(n_uly):
            there = blk, n_uly - 1 - u
            if 0 <= other < n_blk // blks:
                there = other * blks + blk % blks, u
            route.append((blk * n_uly + u, there[0] * n_uly + there[1]))
    return route


def row_pairs(n_groups, n_blk, n_uly):
    route = []
    size = n_blk * n_uly
    for g in range(n_groups):
        for i in range(size):
            h = i % TH
            if h == 1:
                there = g * size + i + 1
            elif h == 2:
                there = g * size + i - 1
            else:
                there = (g + 1) % n_groups * size + i
            route.append((g * size + i, there))
    return route


def place():
    n_uly = lax.axis_size("uly")
    rows = TH // n_uly
    blk = lax.axis_index("blk")
    row = lax.rem(blk, rows) * n_uly + lax.axis_index("uly")
    return lax.rem(lax.div(blk, rows), 2), row, (row > 0) & (row < TH - 1)


def flag_rows(keep, parity, key_row, query_row):
    first = lax.broadcasted_iota(jnp.int32, (1, HD), 1) < TILE
    tiles = keep.shape[0]
    line = lax.rem(query_row * TW, tiles)
    base = (keep.shape[1] - tiles) // 2
    step = 1 - 2 * parity
    rows = []
    for dt in (0, step, -step):
        column = base + TH * TW * dt + TW * (key_row - query_row) + line
        for w in range(TW):
            col = jnp.clip(column + w, 0, keep.shape[1] - 1)
            low = (keep[line, col] > 0).astype(jnp.float32)
            high = (keep[line + 1, col] > 0).astype(jnp.float32)
            rows.append(jnp.where(first, low, high))
    return rows


def prepare_kernel(keep_hbm, q_hbm, bias, q_out, keep, sems):
    tokens = q_hbm.shape[0]
    flags = pltpu.make_async_copy(keep_hbm, keep, sems.at[0])
    flags.start()
    copy = pltpu.make_async_copy(q_hbm, q_out.at[:tokens], sems.at[1])
    copy.start()
    flags.wait()
    parity, row, _ = place()
    sibling = row + 1 - 2 * lax.rem(row, 2)
    across = jnp.where(row < TH // 2, row + 1, row - 1)
    rows = flag_rows(keep, parity, row, row) + flag_rows(keep, parity, row, sibling)
    rows += [jnp.ones((1, HD), jnp.float32)] * (bias.shape[0] - len(rows))
    bias[...] = (jnp.concatenate(rows, axis=0) - 1.0) * -FILL
    rows = flag_rows(keep, parity, across, row)
    rows += [jnp.zeros((1, HD), jnp.float32)] * (FLAG_ROWS - len(rows))
    q_out[tokens:, :HD] = jnp.concatenate(rows, axis=0).astype(q_out.dtype)
    copy.wait()


def unit(h, q, keys, flags, p_ref, st_ref, src):
    scale = LOG2E / math.sqrt(HD)
    s = lax.dot_general(keys, q, (((1,), (1,)), ((), ())), preferred_element_type=jnp.float32)
    t = jnp.concatenate([s[n * TILE : (n + 1) * TILE] * scale + flag for n, flag in enumerate(flags)], axis=0)
    m = jnp.max(t, axis=0, keepdims=True)
    e = jnp.exp2(t - m)
    p_ref[h, :, src * HD : (src + 1) * HD] = e.astype(jnp.bfloat16)
    st_ref[src, h : h + 1, :] = m
    st_ref[src, STAT + h : STAT + h + 1, :] = jnp.sum(e, axis=0, keepdims=True)


def all_heads(qs, ks, flags, p_ref, st_ref):
    rows = ks[0].shape[0]
    st_ref[...] = jnp.ones_like(st_ref)
    for h in range(p_ref.shape[0]):
        cols = pl.ds(h * HD, HD)
        keys = jnp.concatenate([k[:, cols] for k in ks], axis=0)
        for src, q in enumerate(qs):
            unit(h, q[:rows, cols], keys, flags[src], p_ref, st_ref, src)


def bias_rows(bias, src, planes):
    return [bias[(src * 3 + n) * TW + w : (src * 3 + n) * TW + w + 1, :] for n in planes for w in range(TW)]


def own_scores_kernel(bias, k_hbm, v_hbm, q_own, q_d, p, st, k_own, v_a, v_b, sems):
    copies = [
        pltpu.make_async_copy(k_hbm, k_own, sems.at[0]),
        pltpu.make_async_copy(v_hbm.at[:, : v_a.shape[1]], v_a, sems.at[1]),
        pltpu.make_async_copy(v_hbm.at[:, v_a.shape[1] :], v_b, sems.at[2]),
    ]
    for copy in copies:
        copy.start()
    for copy in copies:
        copy.wait()
    all_heads((q_own, q_d), (k_own,), [bias_rows(bias, src, (0,)) for src in range(2)], p, st)


def near_scores_kernel(bias, k_e, k_o, q_own, q_d, p, st):
    all_heads((q_own, q_d), (k_e, k_o), [bias_rows(bias, src, (1, 2)) for src in range(2)], p, st)


def far_scores_kernel(k_own, k_e, k_o, q_x, p, st):
    _, _, inner = place()

    @pl.when(inner)
    def _():
        tokens = k_own.shape[0]
        flags = (q_x[tokens:, :HD].astype(jnp.float32) - 1.0) * -FILL
        all_heads((q_x,), (k_own, k_e, k_o), [[flags[n : n + 1] for n in range(3 * TW)]], p, st)


def split(values, pieces):
    out = []
    for _ in range(pieces):
        piece = values.astype(jnp.bfloat16).astype(jnp.float32)
        out.append(piece)
        values = values - piece
    return out


def stat_rows(heads):
    return -(-5 * heads // 16) * 16


def put_stats(o_ref, peak, total):
    at = o_ref.shape[0] - stat_rows(peak.shape[0])
    rows = split(peak, 3) + split(total, 2)
    spare = o_ref.shape[0] - at - 5 * peak.shape[0]
    if spare:
        rows.append(jnp.zeros((spare, HD), jnp.float32))
    o_ref[at:, :] = jnp.concatenate(rows, axis=0).astype(jnp.bfloat16)


def get_stats(o_ref, heads):
    rows = o_ref[o_ref.shape[0] - stat_rows(heads) :, :].astype(jnp.float32)
    part = [rows[n * heads : (n + 1) * heads] for n in range(5)]
    return part[0] + part[1] + part[2], part[3] + part[4]


def weigh(values, p):
    return lax.dot_general(values, p, (((0,), (0,)), ((), ())), preferred_element_type=jnp.float32)


def far_values_kernel(heads, p, st, v_own, v_e, v_o, o_x):
    _, _, inner = place()
    lo, hi = heads[0], heads[-1] + 1

    @pl.when(inner)
    def _():
        total = st[0, STAT + lo : STAT + hi]
        put_stats(o_x, st[0, lo:hi], total)
        factor = 1.0 / total
        for n, h in enumerate(heads):
            cols = pl.ds(n * HD, HD)
            values = jnp.concatenate([v_own[:, cols], v_e[:, cols], v_o[:, cols]], axis=0)
            o_x[cols, :] = (weigh(values, p[h]) * factor[n : n + 1]).astype(o_x.dtype)


def merge(st_0, st_1, src):
    m0, l0, m1, l1 = st_0[src, :STAT], st_0[src, STAT:], st_1[src, :STAT], st_1[src, STAT:]
    peak = jnp.maximum(m0, m1)
    f0, f1 = jnp.exp2(m0 - peak), jnp.exp2(m1 - peak)
    total = f0 * l0 + f1 * l1
    return peak, total, (f0 / total, f1 / total)


def near_values_kernel(heads, every, p_0, p_1, st_0, st_1, v_own, v_e, v_o, o_own, o_d, *st_own):
    own = merge(st_0, st_1, 0)
    sib = merge(st_0, st_1, 1)
    if st_own:
        st_own[0][:STAT] = own[0]
        st_own[0][STAT:] = own[1]
        put_stats(o_d, sib[0][:every], sib[1][:every])
    for n, h in enumerate(heads):
        cols = pl.ds(n * HD, HD)
        beside = jnp.concatenate([v_e[:, cols], v_o[:, cols]], axis=0)
        part_0, part_1 = weigh(v_own[:, cols], p_0[h]), weigh(beside, p_1[h])
        for src, (out, factors) in enumerate(((o_own, own[2]), (o_d, sib[2]))):
            lanes = slice(src * HD, (src + 1) * HD)
            o = part_0[:, lanes] * factors[0][h : h + 1] + part_1[:, lanes] * factors[1][h : h + 1]
            out[cols, :] = o.astype(out.dtype)


def combine_kernel(heads, every, o_own, o_x, o_d, sib, st_own, *refs):
    out, buf, sem = refs[-3:]
    _, _, inner = place()
    lo, hi = heads[0], heads[-1] + 1
    m0, l0 = st_own[lo:hi], st_own[STAT + lo : STAT + hi]
    m1, l1 = [v[lo:hi] for v in get_stats(sib, every)]
    m2, l2 = get_stats(o_x, len(heads))
    m2, l2 = jnp.where(inner, m2, FILL), jnp.where(inner, l2, 0.0)
    peak = jnp.maximum(jnp.maximum(m0, m1), m2)
    f0, f1, f2 = l0 * jnp.exp2(m0 - peak), l1 * jnp.exp2(m1 - peak), l2 * jnp.exp2(m2 - peak)
    total = f0 + f1 + f2
    w0, w1, w2 = f0 / total, f1 / total, f2 / total
    for n in range(len(heads)):
        cols = pl.ds(n * HD, HD)
        x = jnp.where(inner, o_x[cols, :].astype(jnp.float32), 0.0)
        o = o_own[cols, :] * w0[n : n + 1] + o_d[cols, :].astype(jnp.float32) * w1[n : n + 1] + x * w2[n : n + 1]
        buf[:, cols] = o.T.astype(buf.dtype)
    copy = pltpu.make_async_copy(buf, out.at[:, lo * HD : hi * HD], sem)
    copy.start()
    copy.wait()


def body(n_groups, query, key, value, keep):
    n_blk, n_uly = lax.axis_size("blk"), lax.axis_size("uly")
    rows, width = query.shape
    heads = width // HD
    first = heads * 7 // 12
    heads_a, heads_b = range(first), range(first, heads)
    wide_a, wide_b = len(heads_a) * HD, len(heads_b) * HD
    everyone = ("groups", "blk", "uly")
    cross = row_pairs(n_groups, n_blk, n_uly)
    cores = [(0, 1), (1, 0)]
    vmem, hbm = pl.BlockSpec(memory_space=pltpu.VMEM), pl.BlockSpec(memory_space=pltpu.HBM)
    bf16, f32 = jnp.bfloat16, jnp.float32

    def exchange(x, parity):
        return lax.ppermute(x, ("blk", "uly"), plane_pairs(n_blk, n_uly, parity))

    def call(kernel, name, us, in_specs, out_shape, scratch=(), out_specs=None, aliases=None):
        return pl.pallas_call(
            kernel,
            in_specs=in_specs,
            out_specs=out_specs or jax.tree.map(lambda _: vmem, out_shape),
            out_shape=out_shape,
            scratch_shapes=scratch,
            input_output_aliases=aliases or {},
            compiler_params=pltpu.CompilerParams(vmem_limit_bytes=16 * 1024 * 1024),
            cost_estimate=pl.CostEstimate(flops=int(us * 1e9), bytes_accessed=0, transcendentals=0),
            name=name,
        )

    def array(dtype, *shape):
        return jax.ShapeDtypeStruct(shape, dtype)

    k_e = exchange(key, 0)
    k_o = exchange(key, 1)
    q_d = lax.ppermute(query, "uly", cores)
    q_late, _ = lax.optimization_barrier((query, q_d))
    bias, q_own = call(
        prepare_kernel,
        "prepare",
        0.7,
        [hbm, hbm],
        [array(f32, 16, HD), array(bf16, rows + FLAG_ROWS, width)],
        [pltpu.SMEM(keep.shape, keep.dtype), pltpu.SemaphoreType.DMA((2,))],
    )(keep, q_late)
    q_x = lax.ppermute(q_own, everyone, cross)

    st_near = array(f32, 2, 2 * STAT, rows)
    p_0, st_0, k_own, v_a, v_b = call(
        own_scores_kernel,
        "own_scores",
        1.5,
        [vmem, hbm, hbm, vmem, vmem],
        [array(bf16, heads, rows, 2 * rows), st_near]
        + [array(bf16, rows, width), array(bf16, rows, wide_a), array(bf16, rows, wide_b)],
        [pltpu.SemaphoreType.DMA((3,))],
    )(bias, key, value, q_own, q_d)

    va_e = exchange(v_a, 0)
    va_o = exchange(v_a, 1)
    v_even, k_e, _ = lax.optimization_barrier((v_b, k_e, st_0))
    vb_e = exchange(v_even, 0)

    p_1, st_1 = call(near_scores_kernel, "near_scores", 2, [vmem] * 5, [array(bf16, heads, 2 * rows, 2 * rows), st_near])(
        bias, k_e, k_o, q_own, q_d
    )
    v_odd, q_x, _ = lax.optimization_barrier((v_b, q_x, st_1))
    vb_o = exchange(v_odd, 1)
    p_x, st_x = call(
        far_scores_kernel, "far_scores", 0, [vmem] * 4, [array(bf16, heads, 3 * rows, rows), array(f32, 1, 2 * STAT, rows)]
    )(k_own, k_e, k_o, q_x)

    va_e, va_o, _ = lax.optimization_barrier((va_e, va_o, st_x))
    xa = call(
        functools.partial(far_values_kernel, heads_a),
        "far_values_a",
        0,
        [vmem] * 5,
        array(bf16, wide_a + stat_rows(len(heads_a)), rows),
    )(p_x, st_x, v_a, va_e, va_o)
    back_xa = lax.ppermute(xa, everyone, cross)
    va_e, va_o, _ = lax.optimization_barrier((va_e, va_o, xa))
    own_a, da, st_own = call(
        functools.partial(near_values_kernel, heads_a, heads),
        "near_values_a",
        0,
        [vmem] * 7,
        [array(f32, wide_a, rows), array(bf16, wide_a + stat_rows(heads), rows), array(f32, 2 * STAT, rows)],
    )(p_0, p_1, st_0, st_1, v_a, va_e, va_o)
    back_da = lax.ppermute(da, "uly", cores)

    vb_e, vb_o, _, _ = lax.optimization_barrier((vb_e, vb_o, st_own, xa))
    xb = call(
        functools.partial(far_values_kernel, heads_b),
        "far_values_b",
        5,
        [vmem] * 5,
        array(bf16, wide_b + stat_rows(len(heads_b)), rows),
    )(p_x, st_x, v_b, vb_e, vb_o)
    back_xb = lax.ppermute(xb, everyone, cross)
    own_b, db = call(
        functools.partial(near_values_kernel, heads_b, heads),
        "near_values_b",
        5,
        [vmem] * 7,
        [array(f32, wide_b, rows), array(bf16, wide_b, rows)],
    )(p_0, p_1, st_0, st_1, v_b, vb_e, vb_o)
    back_db = lax.ppermute(db, "uly", cores)

    out = array(query.dtype, rows, width)
    half = call(
        functools.partial(combine_kernel, heads_a, heads),
        "combine_a",
        0,
        [vmem] * 5,
        out,
        [pltpu.VMEM((rows, wide_a), query.dtype), pltpu.SemaphoreType.DMA],
        hbm,
    )(own_a, back_xa, back_da, back_da, st_own)
    return call(
        functools.partial(combine_kernel, heads_b, heads),
        "combine_b",
        0,
        [vmem] * 5 + [hbm],
        out,
        [pltpu.VMEM((rows, wide_b), query.dtype), pltpu.SemaphoreType.DMA],
        hbm,
        {5: 0},
    )(own_b, back_xb, back_db, back_da, st_own, half)


def solution(mesh):
    tokens = P(("groups", "blk", "uly"), None)
    return jax.shard_map(
        functools.partial(body, mesh.shape["groups"]),
        mesh=mesh,
        in_specs=(tokens, tokens, tokens, P(("groups", "blk"), None)),
        out_specs=tokens,
        check_vma=False,
    )
```

```python
import functools
import math

import jax
import jax.numpy as jnp
from jax import lax
from jax.experimental import pallas as pl
from jax.experimental.pallas import tpu as pltpu
from jax.sharding import PartitionSpec as P

HD = 128
TILE = 64
TH = 4
TW = 2
STAT = 16
FLAG_ROWS = 16
FILL = -1e30
LOG2E = 1.4426950408889634


def plane_pairs(n_blk, n_uly, parity):
    blks = TH // n_uly
    route = []
    for blk in range(n_blk):
        t = blk // blks
        other = t + 1 if t % 2 == parity else t - 1
        for u in range(n_uly):
            there = blk, n_uly - 1 - u
            if 0 <= other < n_blk // blks:
                there = other * blks + blk % blks, u
            route.append((blk * n_uly + u, there[0] * n_uly + there[1]))
    return route


def chip_pairs(n_blk, n_uly):
    blks = TH // n_uly
    return [(blk, blk - blk % blks + blks - 1 - blk % blks) for blk in range(n_blk)]


def place():
    n_uly = lax.axis_size("uly")
    rows = TH // n_uly
    blk = lax.axis_index("blk")
    row = lax.rem(blk, rows) * n_uly + lax.axis_index("uly")
    return lax.rem(lax.div(blk, rows), 2), row, (row > 0) & (row < TH - 1)


def flag_rows(keep, parity, key_row, query_row):
    first = lax.broadcasted_iota(jnp.int32, (1, HD), 1) < TILE
    tiles = keep.shape[0]
    line = lax.rem(query_row * TW, tiles)
    base = (keep.shape[1] - tiles) // 2
    step = 1 - 2 * parity
    rows = []
    for dt in (0, step, -step):
        column = base + TH * TW * dt + TW * (key_row - query_row) + line
        for w in range(TW):
            col = jnp.clip(column + w, 0, keep.shape[1] - 1)
            low = (keep[line, col] > 0).astype(jnp.float32)
            high = (keep[line + 1, col] > 0).astype(jnp.float32)
            rows.append(jnp.where(first, low, high))
    return rows


def by_role(middle, outer):
    _, _, inner = place()
    pl.when(inner)(middle)
    pl.when(jnp.logical_not(inner))(outer)


def my_columns(width, mine=True):
    u = lax.axis_index("uly")
    return pl.ds(pl.multiple_of((u if mine else 1 - u) * width, HD), width)


def cut_kernel(k_hbm, v_hbm, k_own, v_own, sems):
    columns = my_columns(k_own.shape[1])
    copies = [
        pltpu.make_async_copy(x.at[:, columns], out, sems.at[n]) for n, (x, out) in enumerate(((k_hbm, k_own), (v_hbm, v_own)))
    ]
    for copy in copies:
        copy.start()
    for copy in copies:
        copy.wait()


def pack_kernel(k_own, v_own, k_d, v_d, first, k_o, v_o):
    rows, width = k_own.shape

    columns = my_columns(width)

    def middle():
        first[:rows, :] = k_own[...]
        first[rows:, :] = v_own[...]
        k_o[...] = k_d[:, columns]
        v_o[...] = v_d[:, columns]

    def outer():
        first[:rows, :] = k_d[:, columns]
        first[rows:, :] = v_d[:, columns]
        k_o[...] = k_own[...]
        v_o[...] = v_own[...]

    by_role(middle, outer)


def arrange_kernel(keep_hbm, q_hbm, q_d, q_i, q_o, bias, mine, keep, sems):
    tokens, width = q_o.shape
    flags = pltpu.make_async_copy(keep_hbm, keep, sems.at[0])
    flags.start()
    copy = pltpu.make_async_copy(q_hbm.at[:, my_columns(width)], mine, sems.at[1])
    copy.start()
    flags.wait()
    parity, row, inner = place()
    sibling = row + 1 - 2 * lax.rem(row, 2)
    middle_row, outer_row = jnp.where(inner, row, sibling), jnp.where(inner, sibling, row)
    rows = []
    for keys in (middle_row, outer_row):
        for queries in (middle_row, outer_row):
            rows += flag_rows(keep, parity, keys, queries)
    bias[...] = (jnp.concatenate(rows, axis=0) - 1.0) * -FILL
    rows = flag_rows(keep, parity, TH - 1 - middle_row, middle_row)
    rows += [jnp.zeros((1, HD), jnp.float32)] * (FLAG_ROWS - len(rows))
    q_i[tokens:, :HD] = jnp.concatenate(rows, axis=0).astype(q_i.dtype)
    copy.wait()

    def middle():
        q_i[:tokens, :] = mine[...]
        q_o[...] = q_d[:, my_columns(width)]

    def outer():
        q_i[:tokens, :] = q_d[:, my_columns(width)]
        q_o[...] = mine[...]

    by_role(middle, outer)


def softmax_part(q, keys, flags):
    scale = LOG2E / math.sqrt(HD)
    s = lax.dot_general(keys, q, (((1,), (1,)), ((), ())), preferred_element_type=jnp.float32)
    t = jnp.concatenate([s[n * TILE : (n + 1) * TILE] * scale + flag for n, flag in enumerate(flags)], axis=0)
    m = jnp.max(t, axis=0, keepdims=True)
    e = jnp.exp2(t - m)
    return e.astype(jnp.bfloat16), m, jnp.sum(e, axis=0, keepdims=True)


def bias_rows(bias, keys):
    count = 3 * TW
    return [[bias[n : n + 1, :] for n in range(at, at + count)] for at in (2 * keys * count, (2 * keys + 1) * count)]


def far_kernel(first, r_e, r_o, q_x, o_x):
    rows = first.shape[0] // 2
    heads = first.shape[1] // HD
    flags = (q_x[rows:, :HD].astype(jnp.float32) - 1.0) * -FILL
    flags = [flags[n : n + 1] for n in range(3 * TW)]
    peaks, totals = [], []
    for h in range(heads):
        cols = pl.ds(h * HD, HD)
        p, m, total = softmax_part(
            q_x[:rows, cols], jnp.concatenate([x[:rows, cols] for x in (first, r_e, r_o)], axis=0), flags
        )
        o = weigh(jnp.concatenate([x[rows:, cols] for x in (first, r_e, r_o)], axis=0), p)
        o_x[cols, :] = (o / total).astype(o_x.dtype)
        peaks.append(m)
        totals.append(total)
    put_stats(o_x, jnp.concatenate(peaks, axis=0), jnp.concatenate(totals, axis=0))


def middle_kernel(bias, first, r_e, r_o, q_i, q_o, acc, st):
    rows = first.shape[0] // 2
    flags = bias_rows(bias, 0)
    for h in range(first.shape[1] // HD):
        cols = pl.ds(h * HD, HD)
        keys = jnp.concatenate([x[:rows, cols] for x in (first, r_e, r_o)], axis=0)
        values = jnp.concatenate([x[rows:, cols] for x in (first, r_e, r_o)], axis=0)
        for src, q in enumerate((q_i, q_o)):
            p, m, total = softmax_part(q[:rows, cols], keys, flags[src])
            acc[cols, src * HD : (src + 1) * HD] = weigh(values, p)
            st[src, h : h + 1, :] = m
            st[src, STAT + h : STAT + h + 1, :] = total


def outer_scores_kernel(bias, k_own, k_e, k_o, q_i, q_o, p_ref, st):
    rows = k_own.shape[0]
    flags = bias_rows(bias, 1)
    for h in range(p_ref.shape[0]):
        cols = pl.ds(h * HD, HD)
        keys = jnp.concatenate([k[:, cols] for k in (k_own, k_e, k_o)], axis=0)
        for src, q in enumerate((q_i, q_o)):
            p, m, total = softmax_part(q[:rows, cols], keys, flags[src])
            p_ref[h, :, src * HD : (src + 1) * HD] = p
            st[src, h : h + 1, :] = m
            st[src, STAT + h : STAT + h + 1, :] = total


def split(values, pieces):
    out = []
    for _ in range(pieces):
        piece = values.astype(jnp.bfloat16).astype(jnp.float32)
        out.append(piece)
        values = values - piece
    return out


def stat_rows(heads):
    return -(-5 * heads // 16) * 16


def put_stats(o_ref, peak, total):
    at = peak.shape[0] * HD
    rows = split(peak, 3) + split(total, 2)
    spare = o_ref.shape[0] - at - 5 * peak.shape[0]
    if spare:
        rows.append(jnp.zeros((spare, HD), jnp.float32))
    o_ref[at:, :] = jnp.concatenate(rows, axis=0).astype(jnp.bfloat16)


def get_stats(o_ref, heads):
    rows = o_ref[heads * HD :, :].astype(jnp.float32)
    part = [rows[n * heads : (n + 1) * heads] for n in range(5)]
    return part[0] + part[1] + part[2], part[3] + part[4]


def weigh(values, p):
    return lax.dot_general(values, p, (((0,), (0,)), ((), ())), preferred_element_type=jnp.float32)


def scale_parts(parts):
    peak = functools.reduce(jnp.maximum, [m for m, _ in parts])
    scales = [jnp.exp2(m - peak) for m, _ in parts]
    total = sum(f * l for f, (_, l) in zip(scales, parts))
    return [f / total for f in scales]


def outer_values_kernel(p, v_own, v_e, acc):
    rows = v_own.shape[0]
    for h in range(p.shape[0]):
        cols = pl.ds(h * HD, HD)
        acc[cols, :] = weigh(jnp.concatenate([v_own[:, cols], v_e[:, cols]], axis=0), p[h, : 2 * rows, :])


def finish_kernel(mine, p, st_i, st_o, acc, acc_o, v_o, x, out):
    heads = p.shape[0]

    def run(src):
        parts = [(st[src, :heads], st[src, STAT : STAT + heads]) for st in (st_i, st_o)]
        if src == 0:
            parts.append(get_stats(x, heads))
        scale = scale_parts(parts)
        if src == 0:
            scale[2] = scale[2] * parts[2][1]
        lanes = slice(src * HD, (src + 1) * HD)
        for h in range(heads):
            cols = pl.ds(h * HD, HD)
            rest = acc_o[cols, lanes] + weigh(v_o[:, cols], p[h, 2 * v_o.shape[0] :, lanes])
            o = acc[cols, lanes] * scale[0][h : h + 1] + rest * scale[1][h : h + 1]
            if src == 0:
                o = o + x[cols, :].astype(jnp.float32) * scale[2][h : h + 1]
            out[:, cols] = o.T.astype(out.dtype)

    by_role(lambda: run(0 if mine else 1), lambda: run(1 if mine else 0))


def put_kernel(own, back, out, sems):
    width = own.shape[1]
    copies = [
        pltpu.make_async_copy(x, out.at[:, my_columns(width, mine)], sems.at[n])
        for n, (x, mine) in enumerate(((own, True), (back, False)))
    ]
    for copy in copies:
        copy.start()
    for copy in copies:
        copy.wait()


def body(query, key, value, keep):
    n_blk, n_uly = lax.axis_size("blk"), lax.axis_size("uly")
    rows, width = query.shape
    half = width // 2
    heads = half // HD
    cores = [(0, 1), (1, 0)]
    vmem, hbm = pl.BlockSpec(memory_space=pltpu.VMEM), pl.BlockSpec(memory_space=pltpu.HBM)
    bf16, f32 = jnp.bfloat16, jnp.float32

    def exchange(x, parity):
        return lax.ppermute(x, ("blk", "uly"), plane_pairs(n_blk, n_uly, parity))

    def across(x):
        return lax.ppermute(x, "blk", chip_pairs(n_blk, n_uly))

    def swap(x):
        return lax.ppermute(x, "uly", cores)

    def call(kernel, name, us, in_specs, out_shape, scratch=(), out_specs=None):
        return pl.pallas_call(
            kernel,
            in_specs=in_specs,
            out_specs=out_specs or jax.tree.map(lambda _: vmem, out_shape),
            out_shape=out_shape,
            scratch_shapes=scratch,
            compiler_params=pltpu.CompilerParams(vmem_limit_bytes=16 * 1024 * 1024),
            cost_estimate=pl.CostEstimate(flops=int(us * 1e9), bytes_accessed=0, transcendentals=0),
            name=name,
        )

    def array(dtype, *shape):
        return jax.ShapeDtypeStruct(shape, dtype)

    def in_hbm(x):
        return pltpu.with_memory_space_constraint(x, pltpu.HBM)

    part = array(bf16, rows, half)
    dma = pltpu.SemaphoreType.DMA
    stats = array(f32, 2, 2 * STAT, rows)

    k_d, v_d, q_d = swap(key), swap(value), swap(query)
    k_own, v_own = call(cut_kernel, "cut", 1, [hbm] * 2, [part] * 2, [dma((2,))])(in_hbm(key), in_hbm(value))
    first, k_o, v_o = call(pack_kernel, "pack", 0, [vmem] * 4, [array(bf16, 2 * rows, half), part, part])(
        k_own, v_own, k_d, v_d
    )

    r_o, r_e = exchange(first, 1), exchange(first, 0)
    q_d, _ = lax.optimization_barrier((q_d, k_o))
    q_i, q_o, bias = call(
        arrange_kernel,
        "arrange",
        0,
        [hbm, hbm, vmem],
        [array(bf16, rows + FLAG_ROWS, half), part, array(f32, 12 * TW, HD)],
        [pltpu.VMEM((rows, half), bf16), pltpu.SMEM(keep.shape, keep.dtype), dma((2,))],
    )(in_hbm(keep), in_hbm(query), q_d)
    q_x = across(q_i)

    k_late, _ = lax.optimization_barrier((k_o, bias))
    ko_o, ko_e = exchange(k_late, 1), exchange(k_late, 0)

    v_even, r_e = lax.optimization_barrier((v_o, r_e))
    vo_e = exchange(v_even, 0)
    x = call(far_kernel, "far", 0, [vmem] * 4, array(bf16, half + stat_rows(heads), rows))(first, r_e, r_o, q_x)
    v_odd, r_o, r_e, _ = lax.optimization_barrier((v_o, r_o, r_e, x))
    x = across(x)
    vo_o = exchange(v_odd, 1)
    acc, st_i = call(middle_kernel, "middle", 1, [vmem] * 6, [array(f32, half, 2 * rows), stats])(
        bias, first, r_e, r_o, q_i, q_o
    )
    ko_o, ko_e, _ = lax.optimization_barrier((ko_o, ko_e, st_i))
    p_o, st_o = call(outer_scores_kernel, "outer_scores", 1, [vmem] * 6, [array(bf16, heads, 3 * rows, 2 * rows), stats])(
        bias, k_o, ko_e, ko_o, q_i, q_o
    )
    vo_e, _ = lax.optimization_barrier((vo_e, st_o))
    acc_o = call(outer_values_kernel, "outer_values", 1, [vmem] * 3, array(f32, half, 2 * rows))(p_o, v_o, vo_e)
    vo_o, _ = lax.optimization_barrier((vo_o, acc_o))
    parts = p_o, st_i, st_o, acc, acc_o, vo_o, x
    out_sib = call(functools.partial(finish_kernel, False), "finish_sibling", 0, [vmem] * 7, part)(*parts)
    back = swap(out_sib)
    acc, _ = lax.optimization_barrier((acc, out_sib))
    parts = p_o, st_i, st_o, acc, acc_o, vo_o, x
    out_own = call(functools.partial(finish_kernel, True), "finish_own", 0, [vmem] * 7, part)(*parts)
    return call(put_kernel, "put", 0, [vmem] * 2, array(query.dtype, rows, width), [dma((2,))], hbm)(out_own, back)


def solution(mesh):
    tokens = P(("groups", "blk", "uly"), None)
    return jax.shard_map(
        body,
        mesh=mesh,
        in_specs=(tokens, tokens, tokens, P(("groups", "blk"), None)),
        out_specs=tokens,
        check_vma=False,
    )
```

```python
import functools
import math

import jax
import jax.numpy as jnp
from jax import lax
from jax.experimental import pallas as pl
from jax.experimental.pallas import tpu as pltpu
from jax.sharding import PartitionSpec as P

HD = 128
TILE = 64
TH = 4
TW = 2
STAT = 16
FLAG_ROWS = 16
FILL = -1e30
LOG2E = 1.4426950408889634


def plane_pairs(n_blk, n_uly, parity):
    blks = TH // n_uly
    route = []
    for blk in range(n_blk):
        t = blk // blks
        other = t + 1 if t % 2 == parity else t - 1
        for u in range(n_uly):
            there = blk, n_uly - 1 - u
            if 0 <= other < n_blk // blks:
                there = other * blks + blk % blks, u
            route.append((blk * n_uly + u, there[0] * n_uly + there[1]))
    return route


def chip_pairs(n_blk, n_uly):
    blks = TH // n_uly
    return [(blk, blk - blk % blks + blks - 1 - blk % blks) for blk in range(n_blk)]


def place():
    n_uly = lax.axis_size("uly")
    rows = TH // n_uly
    blk = lax.axis_index("blk")
    row = lax.rem(blk, rows) * n_uly + lax.axis_index("uly")
    return lax.rem(lax.div(blk, rows), 2), row, (row > 0) & (row < TH - 1)


def flag_rows(keep, parity, key_row, query_row):
    first = lax.broadcasted_iota(jnp.int32, (1, HD), 1) < TILE
    tiles = keep.shape[0]
    line = lax.rem(query_row * TW, tiles)
    base = (keep.shape[1] - tiles) // 2
    step = 1 - 2 * parity
    rows = []
    for dt in (0, step, -step):
        column = base + TH * TW * dt + TW * (key_row - query_row) + line
        for w in range(TW):
            col = jnp.clip(column + w, 0, keep.shape[1] - 1)
            low = (keep[line, col] > 0).astype(jnp.float32)
            high = (keep[line + 1, col] > 0).astype(jnp.float32)
            rows.append(jnp.where(first, low, high))
    return rows


def by_role(middle, outer):
    _, _, inner = place()
    pl.when(inner)(middle)
    pl.when(jnp.logical_not(inner))(outer)


def my_columns(width, mine=True):
    u = lax.axis_index("uly")
    return pl.ds(pl.multiple_of((u if mine else 1 - u) * width, HD), width)


def cut_kernel(keep_hbm, k_hbm, v_hbm, q_hbm, k_own, v_own, q_own, flags, bias, keep, sems):
    table = pltpu.make_async_copy(keep_hbm, keep, sems.at[3])
    table.start()
    columns = my_columns(k_own.shape[1])
    copies = [
        pltpu.make_async_copy(x.at[:, columns], out, sems.at[n])
        for n, (x, out) in enumerate(((k_hbm, k_own), (v_hbm, v_own), (q_hbm, q_own)))
    ]
    for copy in copies:
        copy.start()
    table.wait()
    parity, row, inner = place()
    sibling = row + 1 - 2 * lax.rem(row, 2)
    middle_row, outer_row = jnp.where(inner, row, sibling), jnp.where(inner, sibling, row)
    rows = []
    for keys in (middle_row, outer_row):
        for queries in (middle_row, outer_row):
            rows += flag_rows(keep, parity, keys, queries)
    bias[...] = (jnp.concatenate(rows, axis=0) - 1.0) * -FILL
    rows = flag_rows(keep, parity, TH - 1 - middle_row, middle_row)
    rows += [jnp.zeros((1, HD), jnp.float32)] * (FLAG_ROWS - len(rows))
    flags[...] = jnp.concatenate(rows, axis=0).astype(flags.dtype)
    for copy in copies:
        copy.wait()


def pack_kernel(k_own, v_own, k_d, v_d, first, k_o, v_o):
    rows, width = k_own.shape

    columns = my_columns(width)

    def middle():
        first[:rows, :] = k_own[...]
        first[rows:, :] = v_own[...]
        k_o[...] = k_d[:, columns]
        v_o[...] = v_d[:, columns]

    def outer():
        first[:rows, :] = k_d[:, columns]
        first[rows:, :] = v_d[:, columns]
        k_o[...] = k_own[...]
        v_o[...] = v_own[...]

    by_role(middle, outer)


def arrange_kernel(flags, q_own, q_d, q_i, q_o):
    tokens, width = q_o.shape
    columns = my_columns(width)
    q_i[tokens:, :HD] = flags[...]

    def middle():
        q_i[:tokens, :] = q_own[...]
        q_o[...] = q_d[:, columns]

    def outer():
        q_i[:tokens, :] = q_d[:, columns]
        q_o[...] = q_own[...]

    by_role(middle, outer)


def softmax_part(q, keys, flags):
    scale = LOG2E / math.sqrt(HD)
    s = lax.dot_general(keys, q, (((1,), (1,)), ((), ())), preferred_element_type=jnp.float32)
    t = jnp.concatenate([s[n * TILE : (n + 1) * TILE] * scale + flag for n, flag in enumerate(flags)], axis=0)
    m = jnp.max(t, axis=0, keepdims=True)
    e = jnp.exp2(t - m)
    return e.astype(jnp.bfloat16), m, jnp.sum(e, axis=0, keepdims=True)


def bias_rows(bias, keys):
    count = 3 * TW
    return [[bias[n : n + 1, :] for n in range(at, at + count)] for at in (2 * keys * count, (2 * keys + 1) * count)]


def join_kernel(first, r_e, keys, values):
    rows = first.shape[0] // 2
    for out, at in ((keys, 0), (values, rows)):
        for n, part in enumerate((first, r_e)):
            out[n * rows : (n + 1) * rows, :] = part[at : at + rows, :]


def far_kernel(keys, values, r_o, q_x, o_x):
    rows = r_o.shape[0] // 2
    flags = (q_x[rows:, :HD].astype(jnp.float32) - 1.0) * -FILL
    flags = [flags[n : n + 1] for n in range(3 * TW)]
    peaks, totals = [], []
    for h in range(keys.shape[1] // HD):
        cols = pl.ds(h * HD, HD)
        p, m, total = softmax_part(q_x[:rows, cols], jnp.concatenate([keys[:, cols], r_o[:rows, cols]], axis=0), flags)
        o = weigh(jnp.concatenate([values[:, cols], r_o[rows:, cols]], axis=0), p)
        o_x[cols, :] = (o / total).astype(o_x.dtype)
        peaks.append(m)
        totals.append(total)
    put_stats(o_x, jnp.concatenate(peaks, axis=0), jnp.concatenate(totals, axis=0))


def middle_kernel(bias, keys, values, r_o, q_i, q_o, acc, st):
    rows = r_o.shape[0] // 2
    flags = bias_rows(bias, 0)
    for h in range(keys.shape[1] // HD):
        cols = pl.ds(h * HD, HD)
        every_key = jnp.concatenate([keys[:, cols], r_o[:rows, cols]], axis=0)
        every_value = jnp.concatenate([values[:, cols], r_o[rows:, cols]], axis=0)
        for src, q in enumerate((q_i, q_o)):
            p, m, total = softmax_part(q[:rows, cols], every_key, flags[src])
            acc[cols, src * HD : (src + 1) * HD] = weigh(every_value, p)
            st[src, h : h + 1, :] = m
            st[src, STAT + h : STAT + h + 1, :] = total


def outer_scores_kernel(bias, k_own, k_e, k_o, q_i, q_o, p_ref, st):
    rows = k_own.shape[0]
    flags = bias_rows(bias, 1)
    for h in range(p_ref.shape[0]):
        cols = pl.ds(h * HD, HD)
        keys = jnp.concatenate([k[:, cols] for k in (k_own, k_e, k_o)], axis=0)
        for src, q in enumerate((q_i, q_o)):
            p, m, total = softmax_part(q[:rows, cols], keys, flags[src])
            p_ref[h, :, src * HD : (src + 1) * HD] = p
            st[src, h : h + 1, :] = m
            st[src, STAT + h : STAT + h + 1, :] = total


def split(values, pieces):
    out = []
    for _ in range(pieces):
        piece = values.astype(jnp.bfloat16).astype(jnp.float32)
        out.append(piece)
        values = values - piece
    return out


def stat_rows(heads):
    return -(-5 * heads // 16) * 16


def put_stats(o_ref, peak, total):
    at = peak.shape[0] * HD
    rows = split(peak, 3) + split(total, 2)
    spare = o_ref.shape[0] - at - 5 * peak.shape[0]
    if spare:
        rows.append(jnp.zeros((spare, HD), jnp.float32))
    o_ref[at:, :] = jnp.concatenate(rows, axis=0).astype(jnp.bfloat16)


def get_stats(o_ref, heads):
    rows = o_ref[heads * HD :, :].astype(jnp.float32)
    part = [rows[n * heads : (n + 1) * heads] for n in range(5)]
    return part[0] + part[1] + part[2], part[3] + part[4]


def weigh(values, p):
    return lax.dot_general(values, p, (((0,), (0,)), ((), ())), preferred_element_type=jnp.float32)


def scale_parts(parts):
    peak = functools.reduce(jnp.maximum, [m for m, _ in parts])
    scales = [jnp.exp2(m - peak) for m, _ in parts]
    total = sum(f * l for f, (_, l) in zip(scales, parts))
    return [f / total for f in scales]


def outer_values_kernel(p, v_own, v_e, acc):
    rows = v_own.shape[0]
    for h in range(p.shape[0]):
        cols = pl.ds(h * HD, HD)
        acc[cols, :] = weigh(jnp.concatenate([v_own[:, cols], v_e[:, cols]], axis=0), p[h, : 2 * rows, :])


def turn_kernel(v, out):
    for h in range(v.shape[1] // HD):
        cols = pl.ds(h * HD, HD)
        out[cols, :] = v[:, cols].T


def finish_kernel(mine, p, st_i, st_o, acc, acc_o, v_t, x, out):
    heads = p.shape[0]

    def run(src):
        parts = [(st[src, :heads], st[src, STAT : STAT + heads]) for st in (st_i, st_o)]
        if src == 0:
            parts.append(get_stats(x, heads))
        scale = scale_parts(parts)
        if src == 0:
            scale[2] = scale[2] * parts[2][1]
        lanes = slice(src * HD, (src + 1) * HD)
        for h in range(heads):
            cols = pl.ds(h * HD, HD)
            rest = jnp.dot(v_t[cols, :], p[h, 2 * v_t.shape[1] :, lanes], preferred_element_type=jnp.float32)
            rest = acc_o[cols, lanes] + rest
            o = acc[cols, lanes] * scale[0][h : h + 1] + rest * scale[1][h : h + 1]
            if src == 0:
                o = o + x[cols, :].astype(jnp.float32) * scale[2][h : h + 1]
            out[:, cols] = o.T.astype(out.dtype)

    by_role(lambda: run(0 if mine else 1), lambda: run(1 if mine else 0))


def put_kernel(own, back, out, sems):
    width = own.shape[1]
    copies = [
        pltpu.make_async_copy(x, out.at[:, my_columns(width, mine)], sems.at[n])
        for n, (x, mine) in enumerate(((own, True), (back, False)))
    ]
    for copy in copies:
        copy.start()
    for copy in copies:
        copy.wait()


def body(query, key, value, keep):
    n_blk, n_uly = lax.axis_size("blk"), lax.axis_size("uly")
    rows, width = query.shape
    half = width // 2
    heads = half // HD
    cores = [(0, 1), (1, 0)]
    vmem, hbm = pl.BlockSpec(memory_space=pltpu.VMEM), pl.BlockSpec(memory_space=pltpu.HBM)
    bf16, f32 = jnp.bfloat16, jnp.float32

    def exchange(x, parity):
        return lax.ppermute(x, ("blk", "uly"), plane_pairs(n_blk, n_uly, parity))

    def across(x):
        return lax.ppermute(x, "blk", chip_pairs(n_blk, n_uly))

    def swap(x):
        return lax.ppermute(x, "uly", cores)

    def call(kernel, name, us, in_specs, out_shape, scratch=(), out_specs=None):
        return pl.pallas_call(
            kernel,
            in_specs=in_specs,
            out_specs=out_specs or jax.tree.map(lambda _: vmem, out_shape),
            out_shape=out_shape,
            scratch_shapes=scratch,
            compiler_params=pltpu.CompilerParams(vmem_limit_bytes=16 * 1024 * 1024),
            cost_estimate=pl.CostEstimate(flops=int(us * 1e9), bytes_accessed=0, transcendentals=0),
            name=name,
        )

    def array(dtype, *shape):
        return jax.ShapeDtypeStruct(shape, dtype)

    def in_hbm(x):
        return pltpu.with_memory_space_constraint(x, pltpu.HBM)

    part = array(bf16, rows, half)
    dma = pltpu.SemaphoreType.DMA
    stats = array(f32, 2, 2 * STAT, rows)

    k_d, v_d, q_d = swap(key), swap(value), swap(query)
    k_own, v_own, q_own, flags, bias = call(
        cut_kernel,
        "cut",
        1,
        [hbm] * 4,
        [part, part, part, array(bf16, FLAG_ROWS, HD), array(f32, 12 * TW, HD)],
        [pltpu.SMEM(keep.shape, keep.dtype), dma((4,))],
    )(in_hbm(keep), in_hbm(key), in_hbm(value), in_hbm(query))
    first, k_o, v_o = call(pack_kernel, "pack", 0, [vmem] * 4, [array(bf16, 2 * rows, half), part, part])(
        k_own, v_own, k_d, v_d
    )

    r_o, r_e = exchange(first, 1), exchange(first, 0)
    q_d, _ = lax.optimization_barrier((q_d, k_o))
    q_i, q_o = call(arrange_kernel, "arrange", 0, [vmem] * 3, [array(bf16, rows + FLAG_ROWS, half), part])(
        flags, q_own, q_d
    )
    q_x = across(q_i)

    k_late, _ = lax.optimization_barrier((k_o, q_o))
    ko_o, ko_e = exchange(k_late, 1), exchange(k_late, 0)

    v_even, q_x = lax.optimization_barrier((v_o, q_x))
    vo_e = exchange(v_even, 0)
    v_odd, r_e = lax.optimization_barrier((v_o, r_e))
    vo_o = exchange(v_odd, 1)
    keys, values = call(join_kernel, "join", 0.1, [vmem] * 2, [array(bf16, 2 * rows, half)] * 2)(first, r_e)
    r_o, _ = lax.optimization_barrier((r_o, values))
    x = call(far_kernel, "far", 0, [vmem] * 4, array(bf16, half + stat_rows(heads), rows))(keys, values, r_o, q_x)
    x = across(x)
    acc, st_i = call(middle_kernel, "middle", 0, [vmem] * 6, [array(f32, half, 2 * rows), stats])(
        bias, keys, values, r_o, q_i, q_o
    )
    ko_o, ko_e, _ = lax.optimization_barrier((ko_o, ko_e, st_i))
    p_o, st_o = call(outer_scores_kernel, "outer_scores", 1, [vmem] * 6, [array(bf16, heads, 3 * rows, 2 * rows), stats])(
        bias, k_o, ko_e, ko_o, q_i, q_o
    )
    vo_e, _ = lax.optimization_barrier((vo_e, st_o))
    acc_o = call(outer_values_kernel, "outer_values", 1, [vmem] * 3, array(f32, half, 2 * rows))(p_o, v_o, vo_e)
    vo_o, _ = lax.optimization_barrier((vo_o, acc_o))
    v_t = call(turn_kernel, "turn", 2, [vmem], array(bf16, half, rows))(vo_o)
    parts = p_o, st_i, st_o, acc, acc_o, v_t, x
    out_sib = call(functools.partial(finish_kernel, False), "finish_sibling", 0, [vmem] * 7, part)(*parts)
    back = swap(out_sib)
    acc, _ = lax.optimization_barrier((acc, out_sib))
    parts = p_o, st_i, st_o, acc, acc_o, v_t, x
    out_own = call(functools.partial(finish_kernel, True), "finish_own", 0, [vmem] * 7, part)(*parts)
    return call(put_kernel, "put", 0, [vmem] * 2, array(query.dtype, rows, width), [dma((2,))], hbm)(out_own, back)


def solution(mesh):
    tokens = P(("groups", "blk", "uly"), None)
    return jax.shard_map(
        body,
        mesh=mesh,
        in_specs=(tokens, tokens, tokens, P(("groups", "blk"), None)),
        out_specs=tokens,
        check_vma=False,
    )
```

```python
import functools
import math

import jax
import jax.numpy as jnp
from jax import lax
from jax.experimental import pallas as pl
from jax.experimental.pallas import tpu as pltpu
from jax.sharding import PartitionSpec as P

HD = 128
TILE = 64
TH = 4
TW = 2
STAT = 16
FLAG_ROWS = 16
FILL = -1e30
LOG2E = 1.4426950408889634


def plane_pairs(n_blk, n_uly, parity):
    blks = TH // n_uly
    route = []
    for blk in range(n_blk):
        t = blk // blks
        other = t + 1 if t % 2 == parity else t - 1
        for u in range(n_uly):
            there = blk, n_uly - 1 - u
            if 0 <= other < n_blk // blks:
                there = other * blks + blk % blks, u
            route.append((blk * n_uly + u, there[0] * n_uly + there[1]))
    return route


def chip_pairs(n_blk, n_uly):
    blks = TH // n_uly
    return [(blk, blk - blk % blks + blks - 1 - blk % blks) for blk in range(n_blk)]


def place():
    n_uly = lax.axis_size("uly")
    rows = TH // n_uly
    blk = lax.axis_index("blk")
    row = lax.rem(blk, rows) * n_uly + lax.axis_index("uly")
    return lax.rem(lax.div(blk, rows), 2), row, (row > 0) & (row < TH - 1)


def flag_rows(keep, parity, key_row, query_row):
    first = lax.broadcasted_iota(jnp.int32, (1, HD), 1) < TILE
    tiles = keep.shape[0]
    line = lax.rem(query_row * TW, tiles)
    base = (keep.shape[1] - tiles) // 2
    step = 1 - 2 * parity
    rows = []
    for dt in (0, step, -step):
        column = base + TH * TW * dt + TW * (key_row - query_row) + line
        for w in range(TW):
            col = jnp.clip(column + w, 0, keep.shape[1] - 1)
            low = (keep[line, col] > 0).astype(jnp.float32)
            high = (keep[line + 1, col] > 0).astype(jnp.float32)
            rows.append(jnp.where(first, low, high))
    return rows


def by_role(middle, outer):
    _, _, inner = place()
    pl.when(inner)(middle)
    pl.when(jnp.logical_not(inner))(outer)


def my_columns(width, mine=True):
    u = lax.axis_index("uly")
    return pl.ds(pl.multiple_of((u if mine else 1 - u) * width, HD), width)


def cut_kernel(keep_hbm, k_hbm, v_hbm, q_hbm, k_own, v_own, q_own, flags, bias, keep, sems):
    table = pltpu.make_async_copy(keep_hbm, keep, sems.at[3])
    table.start()
    columns = my_columns(k_own.shape[1])
    copies = [
        pltpu.make_async_copy(x.at[:, columns], out, sems.at[n])
        for n, (x, out) in enumerate(((k_hbm, k_own), (v_hbm, v_own), (q_hbm, q_own)))
    ]
    for copy in copies:
        copy.start()
    table.wait()
    parity, row, inner = place()
    sibling = row + 1 - 2 * lax.rem(row, 2)
    middle_row, outer_row = jnp.where(inner, row, sibling), jnp.where(inner, sibling, row)
    rows = []
    for keys in (middle_row, outer_row):
        for queries in (middle_row, outer_row):
            rows += flag_rows(keep, parity, keys, queries)
    bias[...] = (jnp.concatenate(rows, axis=0) - 1.0) * -FILL
    rows = flag_rows(keep, parity, TH - 1 - middle_row, middle_row)
    rows += [jnp.zeros((1, HD), jnp.float32)] * (FLAG_ROWS - len(rows))
    flags[...] = jnp.concatenate(rows, axis=0).astype(flags.dtype)
    for copy in copies:
        copy.wait()


def pack_kernel(k_own, v_own, k_d, v_d, first, k_o, v_o):
    rows, width = k_own.shape

    columns = my_columns(width)

    def middle():
        first[:rows, :] = k_own[...]
        first[rows:, :] = v_own[...]
        k_o[...] = k_d[:, columns]
        v_o[...] = v_d[:, columns]

    def outer():
        first[:rows, :] = k_d[:, columns]
        first[rows:, :] = v_d[:, columns]
        k_o[...] = k_own[...]
        v_o[...] = v_own[...]

    by_role(middle, outer)


def arrange_kernel(flags, q_own, q_d, q_i, q_o):
    tokens, width = q_o.shape
    columns = my_columns(width)
    q_i[tokens:, :HD] = flags[...]

    def middle():
        q_i[:tokens, :] = q_own[...]
        q_o[...] = q_d[:, columns]

    def outer():
        q_i[:tokens, :] = q_d[:, columns]
        q_o[...] = q_own[...]

    by_role(middle, outer)


def softmax_part(q, keys, flags):
    scale = LOG2E / math.sqrt(HD)
    s = lax.dot_general(keys, q, (((1,), (1,)), ((), ())), preferred_element_type=jnp.float32)
    t = jnp.concatenate([s[n * TILE : (n + 1) * TILE] * scale + flag for n, flag in enumerate(flags)], axis=0)
    m = jnp.max(t, axis=0, keepdims=True)
    e = jnp.exp2(t - m)
    return e.astype(jnp.bfloat16), m, jnp.sum(e, axis=0, keepdims=True)


def bias_rows(bias, keys):
    count = 3 * TW
    return [[bias[n : n + 1, :] for n in range(at, at + count)] for at in (2 * keys * count, (2 * keys + 1) * count)]


def join_kernel(first, r_e, keys, values):
    rows = first.shape[0] // 2
    for out, at in ((keys, 0), (values, rows)):
        for n, part in enumerate((first, r_e)):
            out[n * rows : (n + 1) * rows, :] = part[at : at + rows, :]


def far_kernel(keys, values, r_o, q_x, o_x):
    rows = r_o.shape[0] // 2
    flags = (q_x[rows:, :HD].astype(jnp.float32) - 1.0) * -FILL
    flags = [flags[n : n + 1] for n in range(3 * TW)]
    peaks, totals = [], []
    for h in range(keys.shape[1] // HD):
        cols = pl.ds(h * HD, HD)
        p, m, total = softmax_part(q_x[:rows, cols], jnp.concatenate([keys[:, cols], r_o[:rows, cols]], axis=0), flags)
        o = weigh(jnp.concatenate([values[:, cols], r_o[rows:, cols]], axis=0), p)
        o_x[cols, :] = (o * (1.0 / total)).astype(o_x.dtype)
        peaks.append(m)
        totals.append(total)
    put_stats(o_x, jnp.concatenate(peaks, axis=0), jnp.concatenate(totals, axis=0))


def middle_kernel(bias, keys, values, r_o, q_i, q_o, acc, st):
    rows = r_o.shape[0] // 2
    flags = bias_rows(bias, 0)
    for h in range(keys.shape[1] // HD):
        cols = pl.ds(h * HD, HD)
        every_key = jnp.concatenate([keys[:, cols], r_o[:rows, cols]], axis=0)
        every_value = jnp.concatenate([values[:, cols], r_o[rows:, cols]], axis=0)
        for src, q in enumerate((q_i, q_o)):
            p, m, total = softmax_part(q[:rows, cols], every_key, flags[src])
            acc[cols, src * HD : (src + 1) * HD] = weigh(every_value, p)
            st[src, h : h + 1, :] = m
            st[src, STAT + h : STAT + h + 1, :] = total


def outer_scores_kernel(bias, k_own, k_e, k_o, q_i, q_o, p_ref, st):
    rows = k_own.shape[0]
    flags = bias_rows(bias, 1)
    for h in range(p_ref.shape[0]):
        cols = pl.ds(h * HD, HD)
        keys = jnp.concatenate([k[:, cols] for k in (k_own, k_e, k_o)], axis=0)
        for src, q in enumerate((q_i, q_o)):
            p, m, total = softmax_part(q[:rows, cols], keys, flags[src])
            p_ref[h, :, src * HD : (src + 1) * HD] = p
            st[src, h : h + 1, :] = m
            st[src, STAT + h : STAT + h + 1, :] = total


def split(values, pieces):
    out = []
    for _ in range(pieces):
        piece = values.astype(jnp.bfloat16).astype(jnp.float32)
        out.append(piece)
        values = values - piece
    return out


def stat_rows(heads):
    return -(-5 * heads // 16) * 16


def put_stats(o_ref, peak, total):
    at = peak.shape[0] * HD
    rows = split(peak, 3) + split(total, 2)
    spare = o_ref.shape[0] - at - 5 * peak.shape[0]
    if spare:
        rows.append(jnp.zeros((spare, HD), jnp.float32))
    o_ref[at:, :] = jnp.concatenate(rows, axis=0).astype(jnp.bfloat16)


def get_stats(o_ref, heads):
    rows = o_ref[heads * HD :, :].astype(jnp.float32)
    part = [rows[n * heads : (n + 1) * heads] for n in range(5)]
    return part[0] + part[1] + part[2], part[3] + part[4]


def weigh(values, p):
    return lax.dot_general(values, p, (((0,), (0,)), ((), ())), preferred_element_type=jnp.float32)


def scale_parts(parts):
    peak = functools.reduce(jnp.maximum, [m for m, _ in parts])
    scales = [jnp.exp2(m - peak) for m, _ in parts]
    total = sum(f * l for f, (_, l) in zip(scales, parts))
    return [f / total for f in scales]


def outer_values_kernel(p, v_own, v_e, acc):
    rows = v_own.shape[0]
    for h in range(p.shape[0]):
        cols = pl.ds(h * HD, HD)
        acc[cols, :] = weigh(jnp.concatenate([v_own[:, cols], v_e[:, cols]], axis=0), p[h, : 2 * rows, :])


def turn_kernel(v, out):
    for h in range(v.shape[1] // HD):
        cols = pl.ds(h * HD, HD)
        out[cols, :] = v[:, cols].T


def finish_kernel(mine, p, st_i, st_o, acc, acc_o, v_t, x, out):
    heads = p.shape[0]

    def run(src):
        parts = [(st[src, :heads], st[src, STAT : STAT + heads]) for st in (st_i, st_o)]
        if src == 0:
            parts.append(get_stats(x, heads))
        scale = scale_parts(parts)
        if src == 0:
            scale[2] = scale[2] * parts[2][1]
        lanes = slice(src * HD, (src + 1) * HD)
        for h in range(heads):
            cols = pl.ds(h * HD, HD)
            rest = jnp.dot(v_t[cols, :], p[h, 2 * v_t.shape[1] :, lanes], preferred_element_type=jnp.float32)
            rest = acc_o[cols, lanes] + rest
            o = acc[cols, lanes] * scale[0][h : h + 1] + rest * scale[1][h : h + 1]
            if src == 0:
                o = o + x[cols, :].astype(jnp.float32) * scale[2][h : h + 1]
            out[:, cols] = o.T.astype(out.dtype)

    by_role(lambda: run(0 if mine else 1), lambda: run(1 if mine else 0))


def put_kernel(mine, x, *refs):
    out, sem = refs[-2:]
    copy = pltpu.make_async_copy(x, out.at[:, my_columns(x.shape[1], mine)], sem)
    copy.start()
    copy.wait()


def body(query, key, value, keep):
    n_blk, n_uly = lax.axis_size("blk"), lax.axis_size("uly")
    rows, width = query.shape
    half = width // 2
    heads = half // HD
    cores = [(0, 1), (1, 0)]
    vmem, hbm = pl.BlockSpec(memory_space=pltpu.VMEM), pl.BlockSpec(memory_space=pltpu.HBM)
    bf16, f32 = jnp.bfloat16, jnp.float32

    def exchange(x, parity):
        return lax.ppermute(x, ("blk", "uly"), plane_pairs(n_blk, n_uly, parity))

    def across(x):
        return lax.ppermute(x, "blk", chip_pairs(n_blk, n_uly))

    def swap(x):
        return lax.ppermute(x, "uly", cores)

    def call(kernel, name, us, in_specs, out_shape, scratch=(), out_specs=None, aliases=None):
        return pl.pallas_call(
            kernel,
            in_specs=in_specs,
            out_specs=out_specs or jax.tree.map(lambda _: vmem, out_shape),
            out_shape=out_shape,
            scratch_shapes=scratch,
            input_output_aliases=aliases or {},
            compiler_params=pltpu.CompilerParams(vmem_limit_bytes=16 * 1024 * 1024),
            cost_estimate=pl.CostEstimate(flops=int(us * 1e9), bytes_accessed=0, transcendentals=0),
            name=name,
        )

    def array(dtype, *shape):
        return jax.ShapeDtypeStruct(shape, dtype)

    def in_hbm(x):
        return pltpu.with_memory_space_constraint(x, pltpu.HBM)

    part = array(bf16, rows, half)
    dma = pltpu.SemaphoreType.DMA
    stats = array(f32, 2, 2 * STAT, rows)

    k_d, v_d, q_d = swap(key), swap(value), swap(query)
    k_own, v_own, q_own, flags, bias = call(
        cut_kernel,
        "cut",
        1,
        [hbm] * 4,
        [part, part, part, array(bf16, FLAG_ROWS, HD), array(f32, 12 * TW, HD)],
        [pltpu.SMEM(keep.shape, keep.dtype), dma((4,))],
    )(in_hbm(keep), in_hbm(key), in_hbm(value), in_hbm(query))
    first, k_o, v_o = call(pack_kernel, "pack", 0, [vmem] * 4, [array(bf16, 2 * rows, half), part, part])(
        k_own, v_own, k_d, v_d
    )

    r_o, r_e = exchange(first, 1), exchange(first, 0)
    q_d, _ = lax.optimization_barrier((q_d, k_o))
    q_i, q_o = call(arrange_kernel, "arrange", 0, [vmem] * 3, [array(bf16, rows + FLAG_ROWS, half), part])(
        flags, q_own, q_d
    )
    q_x = across(q_i)

    k_late, _ = lax.optimization_barrier((k_o, q_o))
    ko_o, ko_e = exchange(k_late, 1), exchange(k_late, 0)

    v_even, q_x = lax.optimization_barrier((v_o, q_x))
    vo_e = exchange(v_even, 0)
    v_odd, r_e = lax.optimization_barrier((v_o, r_e))
    vo_o = exchange(v_odd, 1)
    keys, values = call(join_kernel, "join", 0.1, [vmem] * 2, [array(bf16, 2 * rows, half)] * 2)(first, r_e)
    r_o, _ = lax.optimization_barrier((r_o, values))
    x = call(far_kernel, "far", 0, [vmem] * 4, array(bf16, half + stat_rows(heads), rows))(keys, values, r_o, q_x)
    x = across(x)
    acc, st_i = call(middle_kernel, "middle", 0, [vmem] * 6, [array(f32, half, 2 * rows), stats])(
        bias, keys, values, r_o, q_i, q_o
    )
    ko_o, ko_e, _ = lax.optimization_barrier((ko_o, ko_e, st_i))
    p_o, st_o = call(outer_scores_kernel, "outer_scores", 1, [vmem] * 6, [array(bf16, heads, 3 * rows, 2 * rows), stats])(
        bias, k_o, ko_e, ko_o, q_i, q_o
    )
    vo_e, _ = lax.optimization_barrier((vo_e, st_o))
    acc_o = call(outer_values_kernel, "outer_values", 1, [vmem] * 3, array(f32, half, 2 * rows))(p_o, v_o, vo_e)
    vo_o, _ = lax.optimization_barrier((vo_o, acc_o))
    v_t = call(turn_kernel, "turn", 2, [vmem], array(bf16, half, rows))(vo_o)
    parts = p_o, st_i, st_o, acc, acc_o, v_t, x
    out_sib = call(functools.partial(finish_kernel, False), "finish_sibling", 0, [vmem] * 7, part)(*parts)
    back = swap(out_sib)
    acc, _ = lax.optimization_barrier((acc, out_sib))
    parts = p_o, st_i, st_o, acc, acc_o, v_t, x
    out_own = call(functools.partial(finish_kernel, True), "finish_own", 0, [vmem] * 7, part)(*parts)
    out = array(query.dtype, rows, width)
    mine = call(functools.partial(put_kernel, True), "put_own", 0, [vmem], out, [dma], hbm)(out_own)
    return call(functools.partial(put_kernel, False), "put_back", 0, [vmem, hbm], out, [dma], hbm, {1: 0})(back, mine)


def solution(mesh):
    tokens = P(("groups", "blk", "uly"), None)
    return jax.shard_map(
        body,
        mesh=mesh,
        in_specs=(tokens, tokens, tokens, P(("groups", "blk"), None)),
        out_specs=tokens,
        check_vma=False,
    )
```

```python
import functools
import math

import jax
import jax.numpy as jnp
from jax import lax
from jax.experimental import pallas as pl
from jax.experimental.pallas import tpu as pltpu
from jax.sharding import PartitionSpec as P

HD = 128
TILE = 64
TH = 4
TW = 2
STAT = 16
FLAG_ROWS = 16
FILL = -1e30
LOG2E = 1.4426950408889634


def plane_pairs(n_blk, n_uly, parity):
    blks = TH // n_uly
    route = []
    for blk in range(n_blk):
        t = blk // blks
        other = t + 1 if t % 2 == parity else t - 1
        for u in range(n_uly):
            there = blk, n_uly - 1 - u
            if 0 <= other < n_blk // blks:
                there = other * blks + blk % blks, u
            route.append((blk * n_uly + u, there[0] * n_uly + there[1]))
    return route


def chip_pairs(n_blk, n_uly):
    blks = TH // n_uly
    return [(blk, blk - blk % blks + blks - 1 - blk % blks) for blk in range(n_blk)]


def place():
    n_uly = lax.axis_size("uly")
    rows = TH // n_uly
    blk = lax.axis_index("blk")
    row = lax.rem(blk, rows) * n_uly + lax.axis_index("uly")
    return lax.rem(lax.div(blk, rows), 2), row, (row > 0) & (row < TH - 1)


def flag_rows(keep, parity, key_row, query_row):
    first = lax.broadcasted_iota(jnp.int32, (1, HD), 1) < TILE
    tiles = keep.shape[0]
    line = lax.rem(query_row * TW, tiles)
    base = (keep.shape[1] - tiles) // 2
    step = 1 - 2 * parity
    rows = []
    for dt in (0, step, -step):
        column = base + TH * TW * dt + TW * (key_row - query_row) + line
        for w in range(TW):
            col = jnp.clip(column + w, 0, keep.shape[1] - 1)
            low = (keep[line, col] > 0).astype(jnp.float32)
            high = (keep[line + 1, col] > 0).astype(jnp.float32)
            rows.append(jnp.where(first, low, high))
    return rows


def by_role(middle, outer):
    _, _, inner = place()
    pl.when(inner)(middle)
    pl.when(jnp.logical_not(inner))(outer)


def my_columns(width, mine=True):
    u = lax.axis_index("uly")
    return pl.ds(pl.multiple_of((u if mine else 1 - u) * width, HD), width)


def cut_kernel(keep_hbm, k_hbm, v_hbm, q_hbm, k_own, v_own, q_own, flags, bias, keep, sems):
    table = pltpu.make_async_copy(keep_hbm, keep, sems.at[3])
    table.start()
    columns = my_columns(k_own.shape[1])
    copies = [
        pltpu.make_async_copy(x.at[:, columns], out, sems.at[n])
        for n, (x, out) in enumerate(((k_hbm, k_own), (v_hbm, v_own), (q_hbm, q_own)))
    ]
    for copy in copies:
        copy.start()
    table.wait()
    parity, row, inner = place()
    sibling = row + 1 - 2 * lax.rem(row, 2)
    middle_row, outer_row = jnp.where(inner, row, sibling), jnp.where(inner, sibling, row)
    rows = []
    for keys in (middle_row, outer_row):
        for queries in (middle_row, outer_row):
            rows += flag_rows(keep, parity, keys, queries)
    bias[...] = (jnp.concatenate(rows, axis=0) - 1.0) * -FILL
    rows = flag_rows(keep, parity, TH - 1 - middle_row, middle_row)
    rows += [jnp.zeros((1, HD), jnp.float32)] * (FLAG_ROWS - len(rows))
    flags[...] = jnp.concatenate(rows, axis=0).astype(flags.dtype)
    for copy in copies:
        copy.wait()


def pack_kernel(k_own, v_own, k_d, v_d, first, k_o, v_o):
    rows, width = k_own.shape

    columns = my_columns(width)

    def middle():
        first[:rows, :] = k_own[...]
        first[rows:, :] = v_own[...]
        k_o[...] = k_d[:, columns]
        v_o[...] = v_d[:, columns]

    def outer():
        first[:rows, :] = k_d[:, columns]
        first[rows:, :] = v_d[:, columns]
        k_o[...] = k_own[...]
        v_o[...] = v_own[...]

    by_role(middle, outer)


def arrange_kernel(flags, q_own, q_d, q_i, q_o):
    tokens, width = q_o.shape
    columns = my_columns(width)
    q_i[tokens:, :HD] = flags[...]

    def middle():
        q_i[:tokens, :] = q_own[...]
        q_o[...] = q_d[:, columns]

    def outer():
        q_i[:tokens, :] = q_d[:, columns]
        q_o[...] = q_own[...]

    by_role(middle, outer)


def softmax_part(q, keys, flags):
    scale = LOG2E / math.sqrt(HD)
    s = lax.dot_general(keys, q, (((1,), (1,)), ((), ())), preferred_element_type=jnp.float32)
    t = jnp.concatenate([s[n * TILE : (n + 1) * TILE] * scale + flag for n, flag in enumerate(flags)], axis=0)
    m = jnp.max(t, axis=0, keepdims=True)
    e = jnp.exp2(t - m)
    return e.astype(jnp.bfloat16), m, jnp.sum(e, axis=0, keepdims=True)


def bias_rows(bias, keys):
    count = 3 * TW
    return [[bias[n : n + 1, :] for n in range(at, at + count)] for at in (2 * keys * count, (2 * keys + 1) * count)]


def join_kernel(first, r_e, keys, values):
    rows = first.shape[0] // 2
    for out, at in ((keys, 0), (values, rows)):
        for n, part in enumerate((first, r_e)):
            out[n * rows : (n + 1) * rows, :] = part[at : at + rows, :]


def far_kernel(keys, values, r_o, q_x, o_x):
    rows = r_o.shape[0] // 2
    flags = (q_x[rows:, :HD].astype(jnp.float32) - 1.0) * -FILL
    flags = [flags[n : n + 1] for n in range(3 * TW)]
    peaks, totals = [], []
    for h in range(keys.shape[1] // HD):
        cols = pl.ds(h * HD, HD)
        p, m, total = softmax_part(q_x[:rows, cols], jnp.concatenate([keys[:, cols], r_o[:rows, cols]], axis=0), flags)
        o = weigh(jnp.concatenate([values[:, cols], r_o[rows:, cols]], axis=0), p)
        o_x[cols, :] = (o * (1.0 / total)).astype(o_x.dtype)
        peaks.append(m)
        totals.append(total)
    put_stats(o_x, jnp.concatenate(peaks, axis=0), jnp.concatenate(totals, axis=0))


def middle_kernel(bias, keys, values, r_o, q_i, q_o, acc, st):
    rows = r_o.shape[0] // 2
    flags = bias_rows(bias, 0)
    for h in range(keys.shape[1] // HD):
        cols = pl.ds(h * HD, HD)
        every_key = jnp.concatenate([keys[:, cols], r_o[:rows, cols]], axis=0)
        every_value = jnp.concatenate([values[:, cols], r_o[rows:, cols]], axis=0)
        for src, q in enumerate((q_i, q_o)):
            p, m, total = softmax_part(q[:rows, cols], every_key, flags[src])
            acc[cols, src * HD : (src + 1) * HD] = weigh(every_value, p)
            st[src, h : h + 1, :] = m
            st[src, STAT + h : STAT + h + 1, :] = total


def outer_scores_kernel(bias, k_own, k_e, k_o, q_i, q_o, p_ref, st):
    rows = k_own.shape[0]
    flags = bias_rows(bias, 1)
    for h in range(p_ref.shape[0]):
        cols = pl.ds(h * HD, HD)
        keys = jnp.concatenate([k[:, cols] for k in (k_own, k_e, k_o)], axis=0)
        for src, q in enumerate((q_i, q_o)):
            p, m, total = softmax_part(q[:rows, cols], keys, flags[src])
            p_ref[h, :, src * HD : (src + 1) * HD] = p
            st[src, h : h + 1, :] = m
            st[src, STAT + h : STAT + h + 1, :] = total


def split(values, pieces):
    out = []
    for _ in range(pieces):
        piece = values.astype(jnp.bfloat16).astype(jnp.float32)
        out.append(piece)
        values = values - piece
    return out


def stat_rows(heads):
    return -(-5 * heads // 16) * 16


def put_stats(o_ref, peak, total):
    at = peak.shape[0] * HD
    rows = split(peak, 3) + split(total, 2)
    spare = o_ref.shape[0] - at - 5 * peak.shape[0]
    if spare:
        rows.append(jnp.zeros((spare, HD), jnp.float32))
    o_ref[at:, :] = jnp.concatenate(rows, axis=0).astype(jnp.bfloat16)


def get_stats(o_ref, heads):
    rows = o_ref[heads * HD :, :].astype(jnp.float32)
    part = [rows[n * heads : (n + 1) * heads] for n in range(5)]
    return part[0] + part[1] + part[2], part[3] + part[4]


def weigh(values, p):
    return lax.dot_general(values, p, (((0,), (0,)), ((), ())), preferred_element_type=jnp.float32)


def scale_parts(parts):
    peak = functools.reduce(jnp.maximum, [m for m, _ in parts])
    scales = [jnp.exp2(m - peak) for m, _ in parts]
    total = sum(f * l for f, (_, l) in zip(scales, parts))
    return [f / total for f in scales]


def outer_values_kernel(p, v_own, v_e, acc):
    rows = v_own.shape[0]
    for h in range(p.shape[0]):
        cols = pl.ds(h * HD, HD)
        acc[cols, :] = weigh(jnp.concatenate([v_own[:, cols], v_e[:, cols]], axis=0), p[h, : 2 * rows, :])


def base_kernel(p, st_i, st_o, acc, acc_o, v_o, out, st):
    heads = p.shape[0]
    scales = []
    for src in range(2):
        parts = [(ref[src, :heads], ref[src, STAT : STAT + heads]) for ref in (st_i, st_o)]
        peak = jnp.maximum(parts[0][0], parts[1][0])
        f0, f1 = jnp.exp2(parts[0][0] - peak), jnp.exp2(parts[1][0] - peak)
        total = f0 * parts[0][1] + f1 * parts[1][1]
        st[src, :heads] = peak
        st[src, STAT : STAT + heads] = total
        scales.append((f0 / total, f1 / total))
    for h in range(heads):
        cols = pl.ds(h * HD, HD)
        rest = acc_o[cols, :] + weigh(v_o[:, cols], p[h, 2 * v_o.shape[0] :, :])
        for src, (s0, s1) in enumerate(scales):
            lanes = slice(src * HD, (src + 1) * HD)
            out[cols, lanes] = acc[cols, lanes] * s0[h : h + 1] + rest[:, lanes] * s1[h : h + 1]


def finish_kernel(mine, o, st, x, out):
    heads = out.shape[1] // HD

    def run(src):
        if src == 0:
            m0, l0 = st[0, :heads], st[0, STAT : STAT + heads]
            m1, l1 = get_stats(x, heads)
            scale = scale_parts([(m0, l0), (m1, l1)])
            w0, w1 = scale[0] * l0, scale[1] * l1
        for h in range(heads):
            cols = pl.ds(h * HD, HD)
            part = o[cols, src * HD : (src + 1) * HD]
            if src == 0:
                part = part * w0[h : h + 1] + x[cols, :].astype(jnp.float32) * w1[h : h + 1]
            out[:, cols] = part.T.astype(out.dtype)

    by_role(lambda: run(0 if mine else 1), lambda: run(1 if mine else 0))


def put_kernel(mine, x, *refs):
    out, sem = refs[-2:]
    copy = pltpu.make_async_copy(x, out.at[:, my_columns(x.shape[1], mine)], sem)
    copy.start()
    copy.wait()


def body(query, key, value, keep):
    n_blk, n_uly = lax.axis_size("blk"), lax.axis_size("uly")
    rows, width = query.shape
    half = width // 2
    heads = half // HD
    cores = [(0, 1), (1, 0)]
    vmem, hbm = pl.BlockSpec(memory_space=pltpu.VMEM), pl.BlockSpec(memory_space=pltpu.HBM)
    bf16, f32 = jnp.bfloat16, jnp.float32

    def exchange(x, parity):
        return lax.ppermute(x, ("blk", "uly"), plane_pairs(n_blk, n_uly, parity))

    def across(x):
        return lax.ppermute(x, "blk", chip_pairs(n_blk, n_uly))

    def swap(x):
        return lax.ppermute(x, "uly", cores)

    def call(kernel, name, us, in_specs, out_shape, scratch=(), out_specs=None, aliases=None):
        return pl.pallas_call(
            kernel,
            in_specs=in_specs,
            out_specs=out_specs or jax.tree.map(lambda _: vmem, out_shape),
            out_shape=out_shape,
            scratch_shapes=scratch,
            input_output_aliases=aliases or {},
            compiler_params=pltpu.CompilerParams(vmem_limit_bytes=16 * 1024 * 1024),
            cost_estimate=pl.CostEstimate(flops=int(us * 1e9), bytes_accessed=0, transcendentals=0),
            name=name,
        )

    def array(dtype, *shape):
        return jax.ShapeDtypeStruct(shape, dtype)

    def in_hbm(x):
        return pltpu.with_memory_space_constraint(x, pltpu.HBM)

    part = array(bf16, rows, half)
    dma = pltpu.SemaphoreType.DMA
    stats = array(f32, 2, 2 * STAT, rows)

    k_d, v_d, q_d = swap(key), swap(value), swap(query)
    k_own, v_own, q_own, flags, bias = call(
        cut_kernel,
        "cut",
        1,
        [hbm] * 4,
        [part, part, part, array(bf16, FLAG_ROWS, HD), array(f32, 12 * TW, HD)],
        [pltpu.SMEM(keep.shape, keep.dtype), dma((4,))],
    )(in_hbm(keep), in_hbm(key), in_hbm(value), in_hbm(query))
    first, k_o, v_o = call(pack_kernel, "pack", 0, [vmem] * 4, [array(bf16, 2 * rows, half), part, part])(
        k_own, v_own, k_d, v_d
    )

    r_o, r_e = exchange(first, 1), exchange(first, 0)
    q_d, _ = lax.optimization_barrier((q_d, k_o))
    q_i, q_o = call(arrange_kernel, "arrange", 0, [vmem] * 3, [array(bf16, rows + FLAG_ROWS, half), part])(
        flags, q_own, q_d
    )
    q_x = across(q_i)

    k_late, _ = lax.optimization_barrier((k_o, q_o))
    ko_o, ko_e = exchange(k_late, 1), exchange(k_late, 0)

    v_even, q_x = lax.optimization_barrier((v_o, q_x))
    vo_e = exchange(v_even, 0)
    v_odd, r_e = lax.optimization_barrier((v_o, r_e))
    vo_o = exchange(v_odd, 1)
    keys, values = call(join_kernel, "join", 0.05, [vmem] * 2, [array(bf16, 2 * rows, half)] * 2)(first, r_e)
    r_o, _ = lax.optimization_barrier((r_o, values))
    x = call(far_kernel, "far", 0, [vmem] * 4, array(bf16, half + stat_rows(heads), rows))(keys, values, r_o, q_x)
    x = across(x)
    acc, st_i = call(middle_kernel, "middle", 0, [vmem] * 6, [array(f32, half, 2 * rows), stats])(
        bias, keys, values, r_o, q_i, q_o
    )
    ko_o, ko_e, _ = lax.optimization_barrier((ko_o, ko_e, st_i))
    p_o, st_o = call(outer_scores_kernel, "outer_scores", 0.5, [vmem] * 6, [array(bf16, heads, 3 * rows, 2 * rows), stats])(
        bias, k_o, ko_e, ko_o, q_i, q_o
    )
    vo_e, _ = lax.optimization_barrier((vo_e, st_o))
    acc_o = call(outer_values_kernel, "outer_values", 0.3, [vmem] * 3, array(f32, half, 2 * rows))(p_o, v_o, vo_e)
    vo_o, _ = lax.optimization_barrier((vo_o, acc_o))
    o, st = call(base_kernel, "base", 0.3, [vmem] * 6, [array(f32, half, 2 * rows), stats])(p_o, st_i, st_o, acc, acc_o, vo_o)
    out_sib = call(functools.partial(finish_kernel, False), "finish_sibling", 0, [vmem] * 3, part)(o, st, x)
    back = swap(out_sib)
    o, _ = lax.optimization_barrier((o, out_sib))
    out_own = call(functools.partial(finish_kernel, True), "finish_own", 0, [vmem] * 3, part)(o, st, x)
    out = array(query.dtype, rows, width)
    mine = call(functools.partial(put_kernel, True), "put_own", 0, [vmem], out, [dma], hbm)(out_own)
    return call(functools.partial(put_kernel, False), "put_back", 0, [vmem, hbm], out, [dma], hbm, {1: 0})(back, mine)


def solution(mesh):
    tokens = P(("groups", "blk", "uly"), None)
    return jax.shard_map(
        body,
        mesh=mesh,
        in_specs=(tokens, tokens, tokens, P(("groups", "blk"), None)),
        out_specs=tokens,
        check_vma=False,
    )
```

```python
import functools
import math

import jax
import jax.numpy as jnp
from jax import lax
from jax.experimental import pallas as pl
from jax.experimental.pallas import tpu as pltpu
from jax.sharding import PartitionSpec as P

HD = 128
TILE = 64
TH = 4
TW = 2
STAT = 16
FLAG_ROWS = 16
FILL = -1e30
LOG2E = 1.4426950408889634


def plane_pairs(n_blk, n_uly, parity):
    blks = TH // n_uly
    route = []
    for blk in range(n_blk):
        t = blk // blks
        other = t + 1 if t % 2 == parity else t - 1
        for u in range(n_uly):
            there = blk, n_uly - 1 - u
            if 0 <= other < n_blk // blks:
                there = other * blks + blk % blks, u
            route.append((blk * n_uly + u, there[0] * n_uly + there[1]))
    return route


def chip_pairs(n_blk, n_uly):
    blks = TH // n_uly
    return [(blk, blk - blk % blks + blks - 1 - blk % blks) for blk in range(n_blk)]


def place():
    n_uly = lax.axis_size("uly")
    rows = TH // n_uly
    blk = lax.axis_index("blk")
    row = lax.rem(blk, rows) * n_uly + lax.axis_index("uly")
    return lax.rem(lax.div(blk, rows), 2), row, (row > 0) & (row < TH - 1)


def flag_rows(keep, parity, key_row, query_row):
    first = lax.broadcasted_iota(jnp.int32, (1, HD), 1) < TILE
    tiles = keep.shape[0]
    line = lax.rem(query_row * TW, tiles)
    base = (keep.shape[1] - tiles) // 2
    step = 1 - 2 * parity
    rows = []
    for dt in (0, step, -step):
        column = base + TH * TW * dt + TW * (key_row - query_row) + line
        for w in range(TW):
            col = jnp.clip(column + w, 0, keep.shape[1] - 1)
            low = (keep[line, col] > 0).astype(jnp.float32)
            high = (keep[line + 1, col] > 0).astype(jnp.float32)
            rows.append(jnp.where(first, low, high))
    return rows


def by_role(middle, outer):
    _, _, inner = place()
    pl.when(inner)(middle)
    pl.when(jnp.logical_not(inner))(outer)


def my_columns(width, mine=True):
    u = lax.axis_index("uly")
    return pl.ds(pl.multiple_of((u if mine else 1 - u) * width, HD), width)


def cut_kernel(keep_hbm, k_hbm, v_hbm, q_hbm, k_own, v_own, q_own, flags, bias, keep, sems):
    table = pltpu.make_async_copy(keep_hbm, keep, sems.at[3])
    table.start()
    columns = my_columns(k_own.shape[1])
    copies = [
        pltpu.make_async_copy(x.at[:, columns], out, sems.at[n])
        for n, (x, out) in enumerate(((k_hbm, k_own), (v_hbm, v_own), (q_hbm, q_own)))
    ]
    for copy in copies:
        copy.start()
    table.wait()
    parity, row, inner = place()
    sibling = row + 1 - 2 * lax.rem(row, 2)
    middle_row, outer_row = jnp.where(inner, row, sibling), jnp.where(inner, sibling, row)
    rows = []
    for keys in (middle_row, outer_row):
        for queries in (middle_row, outer_row):
            rows += flag_rows(keep, parity, keys, queries)
    bias[...] = (jnp.concatenate(rows, axis=0) - 1.0) * -FILL
    rows = flag_rows(keep, parity, TH - 1 - middle_row, middle_row)
    rows += [jnp.zeros((1, HD), jnp.float32)] * (FLAG_ROWS - len(rows))
    flags[...] = jnp.concatenate(rows, axis=0).astype(flags.dtype)
    for copy in copies:
        copy.wait()


def pack_kernel(k_own, v_own, k_d, v_d, first, k_o, v_o):
    rows, width = k_own.shape

    columns = my_columns(width)

    def middle():
        first[:rows, :] = k_own[...]
        first[rows:, :] = v_own[...]
        k_o[...] = k_d[:, columns]
        v_o[...] = v_d[:, columns]

    def outer():
        first[:rows, :] = k_d[:, columns]
        first[rows:, :] = v_d[:, columns]
        k_o[...] = k_own[...]
        v_o[...] = v_own[...]

    by_role(middle, outer)


def arrange_kernel(flags, q_own, q_d, q_i, q_o):
    tokens, width = q_o.shape
    columns = my_columns(width)
    q_i[tokens:, :HD] = flags[...]

    def middle():
        q_i[:tokens, :] = q_own[...]
        q_o[...] = q_d[:, columns]

    def outer():
        q_i[:tokens, :] = q_d[:, columns]
        q_o[...] = q_own[...]

    by_role(middle, outer)


def softmax_part(q, keys, flags):
    scale = LOG2E / math.sqrt(HD)
    s = lax.dot_general(keys, q, (((1,), (1,)), ((), ())), preferred_element_type=jnp.float32)
    t = jnp.concatenate([s[n * TILE : (n + 1) * TILE] * scale + flag for n, flag in enumerate(flags)], axis=0)
    m = jnp.max(t, axis=0, keepdims=True)
    e = jnp.exp2(t - m)
    return e.astype(jnp.bfloat16), m, jnp.sum(e, axis=0, keepdims=True)


def bias_rows(bias, keys):
    count = 3 * TW
    return [[bias[n : n + 1, :] for n in range(at, at + count)] for at in (2 * keys * count, (2 * keys + 1) * count)]


def join_kernel(first, r_e, keys, values):
    rows = first.shape[0] // 2
    for out, at in ((keys, 0), (values, rows)):
        for n, part in enumerate((first, r_e)):
            out[n * rows : (n + 1) * rows, :] = part[at : at + rows, :]


def far_kernel(keys, values, r_o, q_x, o_x):
    rows = r_o.shape[0] // 2
    flags = (q_x[rows:, :HD].astype(jnp.float32) - 1.0) * -FILL
    flags = [flags[n : n + 1] for n in range(3 * TW)]
    peaks, totals = [], []
    for h in range(keys.shape[1] // HD):
        cols = pl.ds(h * HD, HD)
        p, m, total = softmax_part(q_x[:rows, cols], jnp.concatenate([keys[:, cols], r_o[:rows, cols]], axis=0), flags)
        o = weigh(jnp.concatenate([values[:, cols], r_o[rows:, cols]], axis=0), p)
        o_x[cols, :] = (o * (1.0 / total)).astype(o_x.dtype)
        peaks.append(m)
        totals.append(total)
    put_stats(o_x, jnp.concatenate(peaks, axis=0), jnp.concatenate(totals, axis=0))


def middle_kernel(bias, keys, values, r_o, q_i, q_o, acc, st):
    rows = r_o.shape[0] // 2
    flags = bias_rows(bias, 0)
    for h in range(keys.shape[1] // HD):
        cols = pl.ds(h * HD, HD)
        every_key = jnp.concatenate([keys[:, cols], r_o[:rows, cols]], axis=0)
        every_value = jnp.concatenate([values[:, cols], r_o[rows:, cols]], axis=0)
        for src, q in enumerate((q_i, q_o)):
            p, m, total = softmax_part(q[:rows, cols], every_key, flags[src])
            acc[cols, src * HD : (src + 1) * HD] = weigh(every_value, p)
            st[src, h : h + 1, :] = m
            st[src, STAT + h : STAT + h + 1, :] = total


def outer_scores_kernel(bias, k_own, k_e, k_o, q_i, q_o, p_ref, st):
    rows = k_own.shape[0]
    flags = bias_rows(bias, 1)
    for h in range(p_ref.shape[0]):
        cols = pl.ds(h * HD, HD)
        keys = jnp.concatenate([k[:, cols] for k in (k_own, k_e, k_o)], axis=0)
        for src, q in enumerate((q_i, q_o)):
            p, m, total = softmax_part(q[:rows, cols], keys, flags[src])
            p_ref[h, :, src * HD : (src + 1) * HD] = p
            st[src, h : h + 1, :] = m
            st[src, STAT + h : STAT + h + 1, :] = total


def split(values, pieces):
    out = []
    for _ in range(pieces):
        piece = values.astype(jnp.bfloat16).astype(jnp.float32)
        out.append(piece)
        values = values - piece
    return out


def stat_rows(heads):
    return -(-5 * heads // 16) * 16


def put_stats(o_ref, peak, total):
    at = peak.shape[0] * HD
    rows = split(peak, 3) + split(total, 2)
    spare = o_ref.shape[0] - at - 5 * peak.shape[0]
    if spare:
        rows.append(jnp.zeros((spare, HD), jnp.float32))
    o_ref[at:, :] = jnp.concatenate(rows, axis=0).astype(jnp.bfloat16)


def get_stats(o_ref, heads):
    rows = o_ref[heads * HD :, :].astype(jnp.float32)
    part = [rows[n * heads : (n + 1) * heads] for n in range(5)]
    return part[0] + part[1] + part[2], part[3] + part[4]


def weigh(values, p):
    return lax.dot_general(values, p, (((0,), (0,)), ((), ())), preferred_element_type=jnp.float32)


def scale_parts(parts):
    peak = functools.reduce(jnp.maximum, [m for m, _ in parts])
    scales = [jnp.exp2(m - peak) for m, _ in parts]
    total = sum(f * l for f, (_, l) in zip(scales, parts))
    return [f / total for f in scales]


def outer_values_kernel(p, v_own, v_e, acc):
    rows = v_own.shape[0]
    for h in range(p.shape[0]):
        cols = pl.ds(h * HD, HD)
        acc[cols, :] = weigh(jnp.concatenate([v_own[:, cols], v_e[:, cols]], axis=0), p[h, : 2 * rows, :])


def base_kernel(p, st_i, st_o, acc, acc_o, v_o, out, st):
    heads = p.shape[0]
    scales = []
    for src in range(2):
        parts = [(ref[src, :heads], ref[src, STAT : STAT + heads]) for ref in (st_i, st_o)]
        peak = jnp.maximum(parts[0][0], parts[1][0])
        f0, f1 = jnp.exp2(parts[0][0] - peak), jnp.exp2(parts[1][0] - peak)
        total = f0 * parts[0][1] + f1 * parts[1][1]
        st[src, :heads] = peak
        st[src, STAT : STAT + heads] = total
        scales.append((f0 / total, f1 / total))
    for h in range(heads):
        cols = pl.ds(h * HD, HD)
        rest = acc_o[cols, :] + weigh(v_o[:, cols], p[h, 2 * v_o.shape[0] :, :])
        for src, (s0, s1) in enumerate(scales):
            lanes = slice(src * HD, (src + 1) * HD)
            out[cols, lanes] = acc[cols, lanes] * s0[h : h + 1] + rest[:, lanes] * s1[h : h + 1]


def finish_kernel(mine, o, st, x, out):
    heads = out.shape[1] // HD

    def run(src):
        if src == 0:
            m0, l0 = st[0, :heads], st[0, STAT : STAT + heads]
            m1, l1 = get_stats(x, heads)
            scale = scale_parts([(m0, l0), (m1, l1)])
            w0, w1 = scale[0] * l0, scale[1] * l1
        for h in range(heads):
            cols = pl.ds(h * HD, HD)
            part = o[cols, src * HD : (src + 1) * HD]
            if src == 0:
                part = part * w0[h : h + 1] + x[cols, :].astype(jnp.float32) * w1[h : h + 1]
            out[:, cols] = part.T.astype(out.dtype)

    by_role(lambda: run(0 if mine else 1), lambda: run(1 if mine else 0))


def finish_own_kernel(o, st, x, out, own, sem):
    finish_kernel(True, o, st, x, own)
    copy = pltpu.make_async_copy(own, out.at[:, my_columns(own.shape[1])], sem)
    copy.start()
    copy.wait()


def put_kernel(x, _, out, sem):
    copy = pltpu.make_async_copy(x, out.at[:, my_columns(x.shape[1], False)], sem)
    copy.start()
    copy.wait()


def body(query, key, value, keep):
    n_blk, n_uly = lax.axis_size("blk"), lax.axis_size("uly")
    rows, width = query.shape
    half = width // 2
    heads = half // HD
    cores = [(0, 1), (1, 0)]
    vmem, hbm = pl.BlockSpec(memory_space=pltpu.VMEM), pl.BlockSpec(memory_space=pltpu.HBM)
    bf16, f32 = jnp.bfloat16, jnp.float32

    def exchange(x, parity):
        return lax.ppermute(x, ("blk", "uly"), plane_pairs(n_blk, n_uly, parity))

    def across(x):
        return lax.ppermute(x, "blk", chip_pairs(n_blk, n_uly))

    def swap(x):
        return lax.ppermute(x, "uly", cores)

    def call(kernel, name, us, in_specs, out_shape, scratch=(), out_specs=None, aliases=None):
        return pl.pallas_call(
            kernel,
            in_specs=in_specs,
            out_specs=out_specs or jax.tree.map(lambda _: vmem, out_shape),
            out_shape=out_shape,
            scratch_shapes=scratch,
            input_output_aliases=aliases or {},
            compiler_params=pltpu.CompilerParams(vmem_limit_bytes=16 * 1024 * 1024),
            cost_estimate=pl.CostEstimate(flops=int(us * 1e9), bytes_accessed=0, transcendentals=0),
            name=name,
        )

    def array(dtype, *shape):
        return jax.ShapeDtypeStruct(shape, dtype)

    def in_hbm(x):
        return pltpu.with_memory_space_constraint(x, pltpu.HBM)

    part = array(bf16, rows, half)
    dma = pltpu.SemaphoreType.DMA
    stats = array(f32, 2, 2 * STAT, rows)

    k_d, v_d, q_d = swap(key), swap(value), swap(query)
    k_own, v_own, q_own, flags, bias = call(
        cut_kernel,
        "cut",
        1,
        [hbm] * 4,
        [part, part, part, array(bf16, FLAG_ROWS, HD), array(f32, 12 * TW, HD)],
        [pltpu.SMEM(keep.shape, keep.dtype), dma((4,))],
    )(in_hbm(keep), in_hbm(key), in_hbm(value), in_hbm(query))
    first, k_o, v_o = call(pack_kernel, "pack", 0, [vmem] * 4, [array(bf16, 2 * rows, half), part, part])(
        k_own, v_own, k_d, v_d
    )

    r_o, r_e = exchange(first, 1), exchange(first, 0)
    q_d, _ = lax.optimization_barrier((q_d, k_o))
    q_i, q_o = call(arrange_kernel, "arrange", 0, [vmem] * 3, [array(bf16, rows + FLAG_ROWS, half), part])(
        flags, q_own, q_d
    )
    q_x = across(q_i)

    k_late, _ = lax.optimization_barrier((k_o, q_o))
    ko_o, ko_e = exchange(k_late, 1), exchange(k_late, 0)

    v_even, q_x = lax.optimization_barrier((v_o, q_x))
    vo_e = exchange(v_even, 0)
    v_odd, r_e = lax.optimization_barrier((v_o, r_e))
    vo_o = exchange(v_odd, 1)
    keys, values = call(join_kernel, "join", 0.05, [vmem] * 2, [array(bf16, 2 * rows, half)] * 2)(first, r_e)
    r_o, _ = lax.optimization_barrier((r_o, values))
    x = call(far_kernel, "far", 0, [vmem] * 4, array(bf16, half + stat_rows(heads), rows))(keys, values, r_o, q_x)
    x = across(x)
    acc, st_i = call(middle_kernel, "middle", 0, [vmem] * 6, [array(f32, half, 2 * rows), stats])(
        bias, keys, values, r_o, q_i, q_o
    )
    ko_o, ko_e, _ = lax.optimization_barrier((ko_o, ko_e, st_i))
    p_o, st_o = call(outer_scores_kernel, "outer_scores", 0.5, [vmem] * 6, [array(bf16, heads, 3 * rows, 2 * rows), stats])(
        bias, k_o, ko_e, ko_o, q_i, q_o
    )
    vo_e, _ = lax.optimization_barrier((vo_e, st_o))
    acc_o = call(outer_values_kernel, "outer_values", 0.3, [vmem] * 3, array(f32, half, 2 * rows))(p_o, v_o, vo_e)
    vo_o, _ = lax.optimization_barrier((vo_o, acc_o))
    o, st = call(base_kernel, "base", 0.3, [vmem] * 6, [array(f32, half, 2 * rows), stats])(p_o, st_i, st_o, acc, acc_o, vo_o)
    out_sib = call(functools.partial(finish_kernel, False), "finish_sibling", 0, [vmem] * 3, part)(o, st, x)
    back = swap(out_sib)
    o, _ = lax.optimization_barrier((o, out_sib))
    out = array(query.dtype, rows, width)
    scratch = [pltpu.VMEM((rows, half), bf16), dma]
    mine = call(finish_own_kernel, "finish_own", 0, [vmem] * 3, out, scratch, hbm)(o, st, x)
    return call(put_kernel, "put_back", 0, [vmem, hbm], out, [dma], hbm, {1: 0})(back, mine)


def solution(mesh):
    tokens = P(("groups", "blk", "uly"), None)
    return jax.shard_map(
        body,
        mesh=mesh,
        in_specs=(tokens, tokens, tokens, P(("groups", "blk"), None)),
        out_specs=tokens,
        check_vma=False,
    )
```
